256 devices in a mesh: segment: 8 (over y, core), vol: 32 (over z, x).
Axes of the slice: x: 4, y: 4, z: 8, core: 2. Of those that a mesh axis runs over, the one named last changes fastest.
Arguments:
- cotangent: bfloat16 [64, 128, 1024], P(None, 'vol'), may hold values from -6 to 6
- labels: int32 [128, 1024], P('vol'), may hold values from 0 to 2
- class_weight: float32 [3], replicated, may hold values from 0.25 to 2
- inputs: bfloat16 [8, 64, 128, 1024], P('segment', None, 'vol'), may hold values from -6 to 6
- fine_pre: bfloat16 [8, 64, 128, 1024], P('segment', None, 'vol'), may hold values from -6 to 6
- pooled: bfloat16 [8, 64, 32, 512], P('segment', None, 'vol'), may hold values from -6 to 6
- coarse_pre: bfloat16 [8, 64, 32, 512], P('segment', None, 'vol'), may hold values from -6 to 6
- fine_filters: bfloat16 [8, 27, 64, 64], P('segment'), may hold values from -0.15625 to 0.15625
- coarse_filters: bfloat16 [8, 27, 64, 64], P('segment'), may hold values from -0.15625 to 0.15625
Outputs:
- input_grads: bfloat16 [8, 64, 128, 1024], P('segment', None, 'vol')
- fine_filter_grads: float32 [8, 27, 64, 64], P('segment')
- coarse_filter_grads: float32 [8, 27, 64, 64], P('segment')
The draws below stay inside these ranges and needn't reach their ends.
Inputs may be any that keep to these rules, and one draw needn't show every extreme that they name: `labels`: 0 is background, 1 fault, 2 horizon.
All inputs are finite; a program needn't handle non-finite values.
Results may differ from the reference program's by a relative error of at most 0.02.
Values may be sent and summed in bfloat16 or wider, within the bound.
No kernel may reach another device: no remote copies, remote signals or barrier semaphores. Data moves between devices by JAX's collectives and lax.ppermute only.
A program may use at most 64 MiB of HBM per device.

```python
import math
import jax
import jax.numpy as jnp
from jax import lax

C = 64
TAPS = 27
CLASSES = 3
XL = 16
SEGMENTS = 8
NDEP = 128
NI = 64
PLANE = 1024
CROWS = 32
CPLANE = 512


def plant(entries, stream_key, least, largest):
    shape = entries.shape
    spot = [jax.random.randint(jax.random.fold_in(stream_key, axis), (), 0, shape[axis]) for axis in range(len(shape))]
    entries = entries.at[tuple(spot)].set(least)
    longest = shape.index(max(shape))
    spot[longest] = (spot[longest] + 1) % shape[longest]
    return entries.at[tuple(spot)].set(largest)


def steps_of(own_key, dims, cuts, least, top_value):
    factor_of, own = 1.0, jax.random.fold_in(own_key, 6)
    for axis_at, parts in cuts:
        draws = jnp.exp(jax.random.uniform(jax.random.fold_in(own, axis_at), (parts,), jnp.float32, least / len(cuts), top_value / len(cuts)))
        factor_of = factor_of * jnp.repeat(draws, dims[axis_at] // parts).reshape([-1 if axis == axis_at else 1 for axis in range(len(dims))])
    return factor_of


def noise(rng, dims, deviation, limit, cuts=(), kind=jnp.bfloat16):
    values = deviation * jax.random.normal(rng, dims, jnp.float32)
    if cuts:
        values = values * steps_of(rng, dims, cuts, -0.22, 0.18)
    return jnp.clip(values, -limit, limit).astype(kind)


def setup_inputs(seed: int = 0) -> dict:
    seeds = jax.random.split(jax.random.key(seed), 10)
    cotangent = noise(seeds[0], (C, NDEP, PLANE), 1.0, 6.0, ((1, 32),))
    labels = plant(jax.random.randint(seeds[1], (NDEP, PLANE), 0, 3), jax.random.fold_in(seeds[1], 1), 0, 2).astype(jnp.int32)
    class_weight = jnp.clip(jnp.exp(jax.random.uniform(seeds[2], (CLASSES,), jnp.float32, math.log(0.25), math.log(2.0))), 0.25, 2.0)
    inputs = noise(seeds[3], (SEGMENTS, C, NDEP, PLANE), 1.0, 6.0, ((0, 8), (2, 32)))
    fine_pre = noise(seeds[4], (SEGMENTS, C, NDEP, PLANE), 1.0, 6.0, ((0, 8), (2, 32)))
    pooled = noise(seeds[5], (SEGMENTS, C, CROWS, CPLANE), 1.0, 6.0, ((0, 8), (2, 32)))
    coarse_pre = noise(seeds[6], (SEGMENTS, C, CROWS, CPLANE), 1.0, 6.0, ((0, 8), (2, 32)))
    fine_filters = noise(seeds[7], (SEGMENTS, TAPS, C, C), (TAPS * C) ** -0.5, 0.15625, ((0, 8),))
    coarse_filters = noise(seeds[8], (SEGMENTS, TAPS, C, C), (TAPS * C) ** -0.5, 0.15625, ((0, 8),))
    return {"cotangent": cotangent, "labels": labels, "class_weight": class_weight, "inputs": inputs, "fine_pre": fine_pre, "pooled": pooled, "coarse_pre": coarse_pre, "fine_filters": fine_filters, "coarse_filters": coarse_filters}


def shift_volume(volume, depth_step, inline_step, cross_step):
    padded = jnp.pad(volume, ((0, 0), (1, 1), (1, 1), (1, 1)))
    depth_len, inline_len, cross_len = (volume.shape[1], volume.shape[2], volume.shape[3])
    return padded[:, 1 - depth_step:1 - depth_step + depth_len, 1 - inline_step:1 - inline_step + inline_len, 1 - cross_step:1 - cross_step + cross_len]

def conv_back(gradient, saved_input, weights):
    kernel = weights.astype(jnp.float32)
    grad_wide = gradient.astype(jnp.float32)
    saved_wide = saved_input.astype(jnp.float32)
    summed = jnp.zeros(grad_wide.shape, jnp.float32)
    filter_list = []
    for tap_index in range(27):
        shifted = shift_volume(grad_wide, tap_index // 9 - 1, tap_index // 3 % 3 - 1, tap_index % 3 - 1)
        summed = summed + jnp.einsum('io,oabc->iabc', kernel[tap_index], shifted, precision=lax.Precision.HIGHEST)
        filter_list.append(jnp.einsum('iabc,oabc->io', saved_wide, shifted, precision=lax.Precision.HIGHEST))
    return (summed, jnp.stack(filter_list))

def reference(cotangent, labels, class_weight, inputs, fine_pre, pooled, coarse_pre, fine_filters, coarse_filters):
    half_depth, half_inline, half_cross = (NDEP // 2, NI // 2, XL // 2)
    fine_scale = 1.0 / math.sqrt(NDEP * NI * XL)
    coarse_scale = 1.0 / math.sqrt(half_depth * half_inline * half_cross)
    cell_weight = class_weight[labels]
    gradient = (cotangent.astype(jnp.float32) * cell_weight[None]).astype(jnp.bfloat16).reshape(C, NDEP, NI, XL)
    grads_out = [None] * SEGMENTS
    fine_out = [None] * SEGMENTS
    coarse_out = [None] * SEGMENTS
    for segment_index in range(SEGMENTS - 1, -1, -1):
        saved_input = inputs[segment_index].reshape(C, NDEP, NI, XL)
        fine_gate = fine_pre[segment_index].reshape(C, NDEP, NI, XL)
        coarse_input = pooled[segment_index].reshape(C, half_inline, half_depth, half_cross).transpose(0, 2, 1, 3)
        coarse_gate = coarse_pre[segment_index].reshape(C, half_inline, half_depth, half_cross).transpose(0, 2, 1, 3)
        grad_wide = gradient.astype(jnp.float32)
        pooled_grad = grad_wide.reshape(C, half_depth, 2, half_inline, 2, half_cross, 2).sum(axis=(2, 4, 6)).astype(jnp.bfloat16)
        coarse_gz = jnp.where(coarse_gate > 0, pooled_grad, jnp.zeros_like(pooled_grad))
        coarse_back, coarse_filt = conv_back(coarse_gz, coarse_input, coarse_filters[segment_index])
        coarse_back = lax.optimization_barrier(coarse_back.astype(jnp.bfloat16)).astype(jnp.float32)
        spread = jnp.broadcast_to(coarse_back[:, :, None, :, None, :, None], (C, half_depth, 2, half_inline, 2, half_cross, 2)).reshape(C, NDEP, NI, XL)
        fine_grad = grad_wide + 0.125 * spread
        fine_gz = jnp.where(fine_gate > 0, fine_grad, jnp.zeros_like(fine_grad)).astype(jnp.bfloat16)
        fine_back, fine_filt = conv_back(fine_gz, saved_input, fine_filters[segment_index])
        gradient = (grad_wide + fine_back).astype(jnp.bfloat16)
        grads_out[segment_index] = gradient.reshape(C, NDEP, NI * XL)
        fine_out[segment_index] = fine_filt * fine_scale
        coarse_out[segment_index] = coarse_filt * coarse_scale
    return (jnp.stack(grads_out), jnp.stack(fine_out), jnp.stack(coarse_out))
```

```python
import functools
import math

import jax
import jax.numpy as jnp
from jax import lax
from jax.experimental import pallas as pl
from jax.experimental.pallas import tpu as pltpu
from jax.sharding import PartitionSpec as P

XL = 16
HX = XL // 2
C = 64
D = 4
NF = 1024
NC = 256
EDGE = NF + 2 * NC
OWN = D * NF + 2 * NC
BF = jnp.bfloat16
F32 = jnp.float32
VMEM_LIMIT = 52 * 1024 * 1024


def spread_matrix():
    coarse = lax.broadcasted_iota(jnp.int32, (NC, NF), 0)
    fine = lax.broadcasted_iota(jnp.int32, (NC, NF), 1)
    owner = (fine // (2 * XL)) * HX + (fine % XL) // 2
    return jnp.where(coarse == owner, 1.0, 0.0).astype(BF)


def filter_matrix(weights):
    grid = weights.reshape(3, 3, 3, C, C)[::-1]
    return jnp.transpose(grid, (1, 3, 0, 2, 4)).reshape(3 * C, 9 * C)


def dot(a, b):
    return jnp.dot(a, b, preferred_element_type=F32)


def dot_nt(a, b):
    return lax.dot_general(a, b, (((1,), (1,)), ((), ())), preferred_element_type=F32)


def store_cross_shifts(store, slab, row, width, columns):
    column = lax.broadcasted_iota(jnp.int32, (C, 128), 1) % columns
    for at in range(0, width, 128):
        part = slab[:, at : at + 128]
        back = jnp.where(column < columns - 1, pltpu.roll(part, 127, 1), 0.0)
        ahead = jnp.where(column > 0, pltpu.roll(part, 1, 1), 0.0)
        store[row : row + C, at : at + 128] = back.astype(BF)
        store[row + C : row + 2 * C, at : at + 128] = part.astype(BF)
        store[row + 2 * C : row + 3 * C, at : at + 128] = ahead.astype(BF)


def inline_sum(taps, columns):
    width = taps.shape[1]
    lane = lax.broadcasted_iota(jnp.int32, (C, width), 1)
    first = jnp.where(lane < width - columns, pltpu.roll(taps[:C], width - columns, 1), 0.0)
    last = jnp.where(lane >= columns, pltpu.roll(taps[2 * C :], columns, 1), 0.0)
    return taps[C : 2 * C] + first + last


def inline_shifts(saved, columns):
    wide = saved.astype(F32)
    width = wide.shape[1]
    lane = lax.broadcasted_iota(jnp.int32, (C, width), 1)
    first = jnp.where(lane >= columns, pltpu.roll(wide, columns, 1), 0.0)
    last = jnp.where(lane < width - columns, pltpu.roll(wide, width - columns, 1), 0.0)
    return jnp.concatenate([first.astype(BF), saved, last.astype(BF)], axis=0)


def write_state(slabs, spread, own_ref, up_ref, down_ref):
    for d in range(D):
        own_ref[:, d * NF : (d + 1) * NF] = slabs[d]
    down_ref[:, :NF] = slabs[0]
    up_ref[:, :NF] = slabs[D - 1]
    for j in range(2):
        pair = dot_nt(jnp.concatenate(slabs[2 * j : 2 * j + 2], axis=0), spread[...])
        pooled = (pair[:C] + pair[C:]).astype(BF)
        own_ref[:, D * NF + j * NC : D * NF + (j + 1) * NC] = pooled
        down_ref[:, NF + j * NC : NF + (j + 1) * NC] = pooled
        up_ref[:, NF + j * NC : NF + (j + 1) * NC] = pooled


def seed_kernel(weight_ref, cot_ref, label_ref, pre_ref, own_ref, up_ref, down_ref, spread_ref):
    spread_ref[...] = spread_matrix()
    slabs = []
    for d in range(D):
        label = label_ref[d : d + 1, :]
        weight = jnp.zeros(label.shape, F32)
        for k in range(3):
            weight = weight + jnp.where(label == k, weight_ref[k], 0.0)
        slabs.append((cot_ref[:, d * NF : (d + 1) * NF].astype(F32) * weight).astype(BF))
    write_state(slabs, spread_ref, own_ref, up_ref, down_ref)
    down_ref[:, EDGE:] = pre_ref[:, :NF]
    up_ref[:, EDGE:] = pre_ref[:, (D - 1) * NF :]


def turn_kernel(*refs):
    (
        act_ref, own_ref, lo_ref, hi_ref, first_lo_ref, first_hi_ref, pre_ref, coarse_pre_ref,
        fine_w_ref, coarse_w_ref, spread_ref,
    ) = refs[:11]
    (
        own_out, up_out, down_out, keep_gz, keep_coarse_gz, keep_grad,
        gz_out, coarse_gz_out, fine_store, coarse_store, sems,
    ) = refs[-11:]

    @pl.when(act_ref[0] == 1)
    def _():
        for j in range(6):
            source = (lo_ref, own_ref, hi_ref)[j // 2]
            base = (NF, D * NF, NF)[j // 2] + (j % 2) * NC
            pooled = source[:, base : base + NC].astype(F32)
            mask = coarse_pre_ref[:, j * NC : (j + 1) * NC].astype(F32) > 0
            gz = jnp.where(mask, pooled, 0.0)
            coarse_gz_out[:, j * NC : (j + 1) * NC] = gz.astype(BF)
            store_cross_shifts(coarse_store, gz, j * 3 * C, NC, HX)
        spreads = []
        for j in range(4):
            taps = dot(coarse_w_ref[...], coarse_store[j * 3 * C : (j + 3) * 3 * C, :])
            back = inline_sum(taps, HX).astype(BF)
            spreads.append(back)
        for d in range(6):
            if d == 0:
                grad = lo_ref[:, :NF]
                pre = first_lo_ref[:, EDGE : EDGE + NF]
            elif d == 5:
                grad = hi_ref[:, :NF]
                pre = first_hi_ref[:, EDGE : EDGE + NF]
            else:
                grad = own_ref[:, (d - 1) * NF : d * NF]
                pre = pre_ref[:, (d - 1) * NF : d * NF]
            spread = dot(spreads[(d + 1) // 2], spread_ref[...])
            total = grad.astype(F32) + 0.125 * spread
            gz = jnp.where(pre.astype(F32) > 0, total, 0.0).astype(BF)
            gz_out[:, d * NF : (d + 1) * NF] = gz
            store_cross_shifts(fine_store, gz.astype(F32), d * 3 * C, NF, XL)
        copies = [
            pltpu.make_async_copy(gz_out, keep_gz, sems.at[0]),
            pltpu.make_async_copy(coarse_gz_out, keep_coarse_gz, sems.at[1]),
        ]
        for copy in copies:
            copy.start()
        slabs = []
        for d in range(D):
            taps = dot(fine_w_ref[...], fine_store[d * 3 * C : (d + 3) * 3 * C, :])
            grad = own_ref[:, d * NF : (d + 1) * NF].astype(F32)
            slabs.append((grad + inline_sum(taps, XL)).astype(BF))
        write_state(slabs, spread_ref, own_out, up_out, down_out)
        last = pltpu.make_async_copy(own_out.at[:, : D * NF], keep_grad, sems.at[2])
        last.start()
        for copy in copies:
            copy.wait()
        last.wait()


def filter_kernel(
    gz_ref, coarse_gz_ref, saved_ref, coarse_saved_ref, out_ref, fine_store, coarse_store
):
    for j in range(1, 5):
        store_cross_shifts(
            coarse_store, coarse_gz_ref[:, j * NC : (j + 1) * NC].astype(F32), (j - 1) * 3 * C, NC, HX
        )
    for d in range(6):
        store_cross_shifts(
            fine_store, gz_ref[:, d * NF : (d + 1) * NF].astype(F32), d * 3 * C, NF, XL
        )
    total = None
    for d in range(D):
        moved = inline_shifts(saved_ref[:, d * NF : (d + 1) * NF], XL)
        term = dot_nt(moved, fine_store[d * 3 * C : (d + 3) * 3 * C, :])
        total = term if total is None else total + term
    out_ref[: 3 * C, :] = total.astype(BF)
    total = None
    for j in range(2):
        moved = inline_shifts(coarse_saved_ref[:, j * NC : (j + 1) * NC], HX)
        term = dot_nt(moved, coarse_store[j * 3 * C : (j + 3) * 3 * C, :])
        total = term if total is None else total + term
    out_ref[3 * C :, :] = total.astype(BF)


VM = pl.BlockSpec(memory_space=pltpu.VMEM)
SM = pl.BlockSpec(memory_space=pltpu.SMEM)
HB = pl.BlockSpec(memory_space=pl.ANY)


def call(kernel, outs, ins, scratch, flops, args, keeps=(), aliases={}):
    moved = sum(a.size * a.dtype.itemsize for a in args)
    return pl.pallas_call(
        kernel,
        out_shape=[jax.ShapeDtypeStruct(shape, BF) for shape in tuple(outs) + tuple(keeps)],
        in_specs=ins,
        out_specs=[VM] * len(outs) + [HB] * len(keeps),
        scratch_shapes=scratch,
        input_output_aliases=aliases,
        compiler_params=pltpu.CompilerParams(vmem_limit_bytes=VMEM_LIMIT),
        cost_estimate=pl.CostEstimate(flops=flops, bytes_accessed=moved, transcendentals=0),
    )(*args)


def depth_slices(array, halo):
    vols = lax.axis_size("vol")
    pairs = array.reshape(C, vols, 2 * HX)
    if halo:
        padded = jnp.pad(pairs, ((0, 0), (1, 1), (0, 0)))
        pairs = jnp.concatenate([padded[:, k : k + vols] for k in range(3)], axis=2)
    moved = lax.all_to_all(pairs, "vol", split_axis=1, concat_axis=1, tiled=True)
    slices = pairs.shape[2] // HX
    moved = moved.reshape(C, vols, slices, HX)
    return jnp.transpose(moved, (0, 2, 1, 3)).reshape(C, slices * vols * HX)


def hop(array, pairs):
    return lax.ppermute(array, ("segment", "vol"), pairs)


def reduce_all(partial):
    vols = lax.axis_size("vol")
    part = partial.reshape(vols, partial.shape[0] // vols, partial.shape[1])
    part = lax.all_to_all(part, "vol", 0, 0)
    part = part.astype(F32).sum(axis=0).astype(BF)
    part = jnp.broadcast_to(part[None], (vols,) + part.shape)
    part = lax.all_to_all(part, "vol", 0, 0)
    return part.reshape(partial.shape)


def filter_order(matrix, scale):
    grid = matrix.reshape(3, C, 3, 3, C)
    grid = jnp.transpose(grid, (2, 0, 3, 1, 4))[::-1].reshape(27, C, C)
    return grid.astype(F32) * scale


def on_device(
    cotangent, labels, class_weight, inputs, fine_pre, pooled, coarse_pre, fine_filters, coarse_filters
):
    segments = lax.axis_size("segment")
    vols = lax.axis_size("vol")
    position = lax.axis_index("segment")
    pre = fine_pre[0].reshape(C, D * NF)
    head_edge = EDGE + NF
    own, up, down, spread = call(
        seed_kernel, [(C, OWN), (C, head_edge), (C, head_edge), (NC, NF)], [SM, VM, VM, VM], [], 10**9,
        (class_weight, cotangent.reshape(C, D * NF), labels, pre),
    )
    first_lo = lax.ppermute(up, "vol", [(v, v + 1) for v in range(vols - 1)])
    first_hi = lax.ppermute(down, "vol", [(v + 1, v) for v in range(vols - 1)])
    coarse_mask = depth_slices(coarse_pre[0], True)
    fine_w = filter_matrix(fine_filters[0])
    coarse_w = filter_matrix(coarse_filters[0])
    coarse_saved = None
    lo, hi = first_lo, first_hi
    keeps = ()
    for turn in range(segments):
        s = segments - 1 - turn
        act = (position == s).astype(jnp.int32).reshape(1)
        own, up, down, *keeps = call(
            turn_kernel,
            [(C, OWN), (C, EDGE), (C, EDGE)],
            [SM] + [VM] * 10 + [HB] * len(keeps),
            [
                pltpu.VMEM((C, 6 * NF), BF), pltpu.VMEM((C, 6 * NC), BF),
                pltpu.VMEM((18 * C, NF), BF), pltpu.VMEM((18 * C, NC), BF), pltpu.SemaphoreType.DMA((3,)),
            ],
            4 * 10**9,
            (act, own, lo, hi, first_lo, first_hi, pre, coarse_mask, fine_w, coarse_w, spread, *keeps),
            ((C, 6 * NF), (C, 6 * NC), (C, D * NF)),
            {11 + k: 3 + k for k in range(len(keeps))},
        )
        if s == 0:
            break
        base, to = s * vols, (s - 1) * vols
        next_lo = hop(up, [(base + v, to + v + 1) for v in range(vols - 1)])
        next_hi = hop(down, [(base + v + 1, to + v) for v in range(vols - 1)])
        next_own = hop(own, [(base + v, to + v) for v in range(vols)])
        if turn == 3:
            saved, own = lax.optimization_barrier((pooled, own))
            coarse_saved = depth_slices(saved[0], False)
            next_lo, next_hi, next_own, coarse_saved = lax.optimization_barrier(
                (next_lo, next_hi, next_own, coarse_saved)
            )
        own, lo, hi = next_own, next_lo, next_hi
    gz, coarse_gz, grad = keeps
    (partial,) = call(
        filter_kernel,
        [(6 * C, 9 * C)],
        [VM] * 4,
        [pltpu.VMEM((18 * C, NF), BF), pltpu.VMEM((12 * C, NC), BF)],
        2 * 10**9,
        (gz, coarse_gz, inputs[0].reshape(C, D * NF), coarse_saved),
    )
    total = reduce_all(partial)
    cells = D * vols * NF
    fine_total = filter_order(total[: 3 * C], 1.0 / math.sqrt(cells))
    coarse_total = filter_order(total[3 * C :], 1.0 / math.sqrt(cells // 8))
    return grad.reshape(1, C, D, NF), fine_total[None], coarse_total[None]


def solution(mesh):
    return jax.shard_map(
        on_device,
        mesh=mesh,
        in_specs=(
            P(None, "vol", None),
            P("vol", None),
            P(),
            P("segment", None, "vol", None),
            P("segment", None, "vol", None),
            P("segment", None, "vol", None),
            P("segment", None, "vol", None),
            P("segment", None, None, None),
            P("segment", None, None, None),
        ),
        out_specs=(
            P("segment", None, "vol", None),
            P("segment", None, None, None),
            P("segment", None, None, None),
        ),
        check_vma=False,
    )
```

```python
import functools
import math

import jax
import jax.numpy as jnp
from jax import lax
from jax.experimental import pallas as pl
from jax.experimental.pallas import tpu as pltpu
from jax.sharding import PartitionSpec as P

XL = 16
HX = XL // 2
C = 64
D = 4
NF = 1024
NC = 256
EDGE = NF + 2 * NC
OWN = D * NF + 2 * NC
BF = jnp.bfloat16
F32 = jnp.float32
VMEM_LIMIT = 51 * 1024 * 1024


def spread_matrix():
    coarse = lax.broadcasted_iota(jnp.int32, (NC, NF), 0)
    fine = lax.broadcasted_iota(jnp.int32, (NC, NF), 1)
    owner = (fine // (2 * XL)) * HX + (fine % XL) // 2
    return jnp.where(coarse == owner, 1.0, 0.0).astype(BF)


def filter_matrix(weights):
    grid = weights.reshape(3, 3, 3, C, C)[::-1]
    return jnp.transpose(grid, (1, 3, 0, 2, 4)).reshape(3 * C, 9 * C)


def dot(a, b):
    return jnp.dot(a, b, preferred_element_type=F32)


def dot_nt(a, b):
    return lax.dot_general(a, b, (((1,), (1,)), ((), ())), preferred_element_type=F32)


def store_cross_shifts(store, slab, row, width, columns):
    column = lax.broadcasted_iota(jnp.int32, (C, 128), 1) % columns
    for at in range(0, width, 128):
        part = slab[:, at : at + 128]
        back = jnp.where(column < columns - 1, pltpu.roll(part, 127, 1), 0.0)
        ahead = jnp.where(column > 0, pltpu.roll(part, 1, 1), 0.0)
        store[row : row + C, at : at + 128] = back.astype(BF)
        store[row + C : row + 2 * C, at : at + 128] = part.astype(BF)
        store[row + 2 * C : row + 3 * C, at : at + 128] = ahead.astype(BF)


def inline_sum(taps, columns):
    width = taps.shape[1]
    lane = lax.broadcasted_iota(jnp.int32, (C, width), 1)
    first = jnp.where(lane < width - columns, pltpu.roll(taps[:C], width - columns, 1), 0.0)
    last = jnp.where(lane >= columns, pltpu.roll(taps[2 * C :], columns, 1), 0.0)
    return taps[C : 2 * C] + first + last


def inline_shifts(saved, columns):
    wide = saved.astype(F32)
    width = wide.shape[1]
    lane = lax.broadcasted_iota(jnp.int32, (C, width), 1)
    first = jnp.where(lane >= columns, pltpu.roll(wide, columns, 1), 0.0)
    last = jnp.where(lane < width - columns, pltpu.roll(wide, width - columns, 1), 0.0)
    return jnp.concatenate([first.astype(BF), saved, last.astype(BF)], axis=0)


def write_state(slabs, spread, own_ref, up_ref, down_ref):
    for d in range(D):
        own_ref[:, d * NF : (d + 1) * NF] = slabs[d]
    down_ref[:, :NF] = slabs[0]
    up_ref[:, :NF] = slabs[D - 1]
    sums = dot_nt(jnp.concatenate(slabs, axis=0), spread[...])
    for j in range(2):
        at = 2 * j * C
        pooled = (sums[at : at + C] + sums[at + C : at + 2 * C]).astype(BF)
        own_ref[:, D * NF + j * NC : D * NF + (j + 1) * NC] = pooled
        down_ref[:, NF + j * NC : NF + (j + 1) * NC] = pooled
        up_ref[:, NF + j * NC : NF + (j + 1) * NC] = pooled


def seed_kernel(weight_ref, cot_ref, label_ref, pre_ref, own_ref, up_ref, down_ref, spread_ref):
    spread_ref[...] = spread_matrix()
    slabs = []
    for d in range(D):
        label = label_ref[d : d + 1, :]
        weight = jnp.zeros(label.shape, F32)
        for k in range(3):
            weight = weight + jnp.where(label == k, weight_ref[k], 0.0)
        slabs.append((cot_ref[:, d * NF : (d + 1) * NF].astype(F32) * weight).astype(BF))
    write_state(slabs, spread_ref, own_ref, up_ref, down_ref)
    down_ref[:, EDGE:] = pre_ref[:, :NF]
    up_ref[:, EDGE:] = pre_ref[:, (D - 1) * NF :]


def turn_kernel(*refs):
    (
        act_ref, own_from, lo_ref, hi_ref, first_lo_ref, first_hi_ref, pre_ref, coarse_pre_ref,
        fine_w_ref, coarse_w_ref, spread_ref,
    ) = refs[:11]
    (
        own_out, up_out, down_out, keep_gz, keep_coarse_gz, keep_grad,
        gz_buf, coarse_gz_buf, fine_store, coarse_store,
        pre_buf, coarse_pre_buf, fine_w, coarse_w, spread, own_ref, sems,
    ) = refs[-17:]

    @pl.when(act_ref[0] == 1)
    def _():
        inner, fine, coarse = pl.ds(NF, D * NF), pl.ds(0, D * NF), pl.ds(D * NF, 2 * NC)
        loads = [
            pltpu.make_async_copy(source, target, sems.at[at])
            for at, (source, target) in enumerate((
                (coarse_pre_ref.at[:, pl.ds(0, 6 * NC)], coarse_pre_buf),
                (coarse_w_ref, coarse_w),
                (spread_ref, spread),
                (first_lo_ref.at[:, pl.ds(EDGE, NF)], pre_buf.at[:, pl.ds(0, NF)]),
                (pre_ref, pre_buf.at[:, inner]),
                (first_hi_ref.at[:, pl.ds(EDGE, NF)], pre_buf.at[:, pl.ds(5 * NF, NF)]),
                (own_from.at[:, fine], own_ref.at[:, fine]),
                (fine_w_ref, fine_w),
                (own_from.at[:, coarse], own_ref.at[:, coarse]),
            ))
        ]
        for load in loads[-1:] + loads[:-1]:
            load.start()
        loads[8].wait()
        loads[0].wait()
        for j in range(6):
            source = (lo_ref, own_ref, hi_ref)[j // 2]
            base = (NF, D * NF, NF)[j // 2] + (j % 2) * NC
            pooled = source[:, base : base + NC].astype(F32)
            mask = coarse_pre_buf[:, j * NC : (j + 1) * NC].astype(F32) > 0
            gz = jnp.where(mask, pooled, 0.0)
            coarse_gz_buf[:, j * NC : (j + 1) * NC] = gz.astype(BF)
            store_cross_shifts(coarse_store, gz, j * 3 * C, NC, HX)
        loads[1].wait()
        backs = []
        for j in range(4):
            taps = dot(coarse_w[...], coarse_store[j * 3 * C : (j + 3) * 3 * C, :])
            backs.append(inline_sum(taps, HX).astype(BF))
        loads[2].wait()
        spreads = dot(jnp.concatenate(backs, axis=0), spread[...])
        for load in loads[3:7]:
            load.wait()
        for d in range(6):
            if d == 0:
                grad = lo_ref[:, :NF]
            elif d == 5:
                grad = hi_ref[:, :NF]
            else:
                grad = own_ref[:, (d - 1) * NF : d * NF]
            j = (d + 1) // 2
            total = grad.astype(F32) + 0.125 * spreads[j * C : (j + 1) * C]
            gz = jnp.where(pre_buf[:, d * NF : (d + 1) * NF].astype(F32) > 0, total, 0.0).astype(BF)
            gz_buf[:, d * NF : (d + 1) * NF] = gz
            store_cross_shifts(fine_store, gz.astype(F32), d * 3 * C, NF, XL)
        saves = [
            pltpu.make_async_copy(gz_buf, keep_gz, sems.at[9]),
            pltpu.make_async_copy(coarse_gz_buf, keep_coarse_gz, sems.at[10]),
        ]
        for save in saves:
            save.start()
        loads[7].wait()
        slabs = []
        for d in range(D):
            taps = dot(fine_w[...], fine_store[d * 3 * C : (d + 3) * 3 * C, :])
            grad = own_ref[:, d * NF : (d + 1) * NF].astype(F32)
            slabs.append((grad + inline_sum(taps, XL)).astype(BF))
        write_state(slabs, spread, own_out, up_out, down_out)
        last = pltpu.make_async_copy(own_out.at[:, pl.ds(0, D * NF)], keep_grad, sems.at[11])
        last.start()
        for save in saves:
            save.wait()
        last.wait()


def filter_kernel(
    gz_ref, coarse_gz_ref, saved_ref, coarse_saved_ref, out_ref, fine_store, coarse_store
):
    for j in range(1, 5):
        store_cross_shifts(
            coarse_store, coarse_gz_ref[:, j * NC : (j + 1) * NC].astype(F32), (j - 1) * 3 * C, NC, HX
        )
    for d in range(6):
        store_cross_shifts(
            fine_store, gz_ref[:, d * NF : (d + 1) * NF].astype(F32), d * 3 * C, NF, XL
        )
    total = None
    for d in range(D):
        moved = inline_shifts(saved_ref[:, d * NF : (d + 1) * NF], XL)
        term = dot_nt(moved, fine_store[d * 3 * C : (d + 3) * 3 * C, :])
        total = term if total is None else total + term
    fine_total, total = total, None
    for j in range(2):
        moved = inline_shifts(coarse_saved_ref[:, (6 + j) * NC : (7 + j) * NC], HX)
        term = dot_nt(moved, coarse_store[j * 3 * C : (j + 3) * 3 * C, :])
        total = term if total is None else total + term
    for inline_tap in range(3):
        for column in range(9):
            depth_tap, cross_tap = 2 - column // 3, column % 3
            tap = depth_tap * 9 + inline_tap * 3 + cross_tap
            rows, lanes = slice(inline_tap * C, (inline_tap + 1) * C), slice(column * C, (column + 1) * C)
            both = jnp.concatenate([fine_total[rows, lanes], total[rows, lanes]], axis=1)
            out_ref[tap * C : (tap + 1) * C, :] = both.astype(BF)


VM = pl.BlockSpec(memory_space=pltpu.VMEM)
SM = pl.BlockSpec(memory_space=pltpu.SMEM)
HB = pl.BlockSpec(memory_space=pl.ANY)


def call(kernel, outs, ins, scratch, flops, args, keeps=(), aliases={}):
    moved = sum(a.size * a.dtype.itemsize for a in args)
    return pl.pallas_call(
        kernel,
        out_shape=[jax.ShapeDtypeStruct(shape, BF) for shape in tuple(outs) + tuple(keeps)],
        in_specs=ins,
        out_specs=[VM] * len(outs) + [HB] * len(keeps),
        scratch_shapes=scratch,
        input_output_aliases=aliases,
        compiler_params=pltpu.CompilerParams(vmem_limit_bytes=VMEM_LIMIT),
        cost_estimate=pl.CostEstimate(flops=flops, bytes_accessed=moved, transcendentals=0),
    )(*args)


def depth_slices(mask, saved, up):
    vols = lax.axis_size("vol")
    pairs = mask.reshape(C, vols, 2 * HX)
    padded = jnp.pad(pairs, ((0, 0), (1, 1), (0, 0)))
    parts = [padded[:, k : k + vols] for k in range(3)] + [saved.reshape(C, vols, 2 * HX)]
    packed, up = lax.optimization_barrier((jnp.concatenate(parts, axis=2), up))
    moved = lax.all_to_all(packed, "vol", split_axis=1, concat_axis=1, tiled=True)
    moved = jnp.transpose(moved.reshape(C, vols, 8, HX), (0, 2, 1, 3)).reshape(C, 8 * NC)
    return moved, up


def hop(array, pairs):
    return lax.ppermute(array, ("segment", "vol"), pairs)


def reduce_all(partial):
    vols = lax.axis_size("vol")
    part = partial.reshape(vols, partial.shape[0] // vols, partial.shape[1])
    part = lax.all_to_all(part, "vol", 0, 0)
    part = part.astype(F32).sum(axis=0).astype(BF)
    part = jnp.broadcast_to(part[None], (vols,) + part.shape)
    part = lax.all_to_all(part, "vol", 0, 0)
    return part.reshape(partial.shape)


def on_device(
    cotangent, labels, class_weight, inputs, fine_pre, pooled, coarse_pre, fine_filters, coarse_filters
):
    segments = lax.axis_size("segment")
    vols = lax.axis_size("vol")
    position = lax.axis_index("segment")
    pre = fine_pre[0].reshape(C, D * NF)
    head_edge = EDGE + NF
    own, up, down, spread = call(
        seed_kernel, [(C, OWN), (C, head_edge), (C, head_edge), (NC, NF)], [SM, VM, VM, VM], [], 10**9,
        (class_weight, cotangent.reshape(C, D * NF), labels, pre),
    )
    coarse_both, up = depth_slices(coarse_pre[0], pooled[0], up)
    first_lo = lax.ppermute(up, "vol", [(v, v + 1) for v in range(vols - 1)])
    first_hi = lax.ppermute(down, "vol", [(v + 1, v) for v in range(vols - 1)])
    fine_w = filter_matrix(fine_filters[0])
    coarse_w = filter_matrix(coarse_filters[0])
    lo, hi = first_lo, first_hi
    keeps = ()
    for turn in range(segments):
        s = segments - 1 - turn
        act = (position == s).astype(jnp.int32).reshape(1)
        own, up, down, *keeps = call(
            turn_kernel,
            [(C, OWN), (C, EDGE), (C, EDGE)],
            [SM, HB, VM, VM] + [HB] * (7 + len(keeps)),
            [
                pltpu.VMEM((C, 6 * NF), BF), pltpu.VMEM((C, 6 * NC), BF),
                pltpu.VMEM((18 * C, NF), BF), pltpu.VMEM((18 * C, NC), BF),
                pltpu.VMEM((C, 6 * NF), BF), pltpu.VMEM((C, 6 * NC), BF),
                pltpu.VMEM((3 * C, 9 * C), BF), pltpu.VMEM((3 * C, 9 * C), BF), pltpu.VMEM((NC, NF), BF),
                pltpu.VMEM((C, OWN), BF), pltpu.SemaphoreType.DMA((12,)),
            ],
            4 * 10**9,
            (act, own, lo, hi, first_lo, first_hi, pre, coarse_both, fine_w, coarse_w, spread, *keeps),
            ((C, 6 * NF), (C, 6 * NC), (C, D * NF)),
            {11 + k: 3 + k for k in range(len(keeps))},
        )
        if s == 0:
            break
        base, to = s * vols, (s - 1) * vols
        next_lo = hop(up, [(base + v, to + v + 1) for v in range(vols - 1)])
        next_hi = hop(down, [(base + v + 1, to + v) for v in range(vols - 1)])
        next_own = hop(own, [(base + v, to + v) for v in range(vols)])
        own, lo, hi = next_own, next_lo, next_hi
    gz, coarse_gz, grad = keeps
    (partial,) = call(
        filter_kernel,
        [(27 * C, 2 * C)],
        [VM] * 4,
        [pltpu.VMEM((18 * C, NF), BF), pltpu.VMEM((12 * C, NC), BF)],
        2 * 10**9,
        (gz, coarse_gz, inputs[0].reshape(C, D * NF), coarse_both),
    )
    total = reduce_all(partial)
    cells = D * vols * NF
    total = total.reshape(27, C, 2 * C).astype(F32)
    fine_total = total[:, :, :C] * (1.0 / math.sqrt(cells))
    coarse_total = total[:, :, C:] * (1.0 / math.sqrt(cells // 8))
    return grad.reshape(1, C, D, NF), fine_total[None], coarse_total[None]


def solution(mesh):
    return jax.shard_map(
        on_device,
        mesh=mesh,
        in_specs=(
            P(None, "vol", None),
            P("vol", None),
            P(),
            P("segment", None, "vol", None),
            P("segment", None, "vol", None),
            P("segment", None, "vol", None),
            P("segment", None, "vol", None),
            P("segment", None, None, None),
            P("segment", None, None, None),
        ),
        out_specs=(
            P("segment", None, "vol", None),
            P("segment", None, None, None),
            P("segment", None, None, None),
        ),
        check_vma=False,
    )
```

```python
import functools
import math

import jax
import jax.numpy as jnp
from jax import lax
from jax.experimental import pallas as pl
from jax.experimental.pallas import tpu as pltpu
from jax.sharding import PartitionSpec as P

XL = 16
HX = XL // 2
C = 64
D = 4
NF = 1024
NC = 256
EDGE = NF + 2 * NC
OWN = D * NF + 2 * NC
BF = jnp.bfloat16
F32 = jnp.float32
VMEM_LIMIT = 52600 * 1024


def spread_matrix():
    coarse = lax.broadcasted_iota(jnp.int32, (NC, NF), 0)
    fine = lax.broadcasted_iota(jnp.int32, (NC, NF), 1)
    owner = (fine // (2 * XL)) * HX + (fine % XL) // 2
    return jnp.where(coarse == owner, 1.0, 0.0).astype(BF)


def filter_matrix(weights):
    grid = weights.reshape(3, 3, 3, C, C)[::-1]
    return jnp.transpose(grid, (1, 3, 0, 2, 4)).reshape(3 * C, 9 * C)


def dot(a, b):
    return jnp.dot(a, b, preferred_element_type=F32)


def dot_nt(a, b):
    return lax.dot_general(a, b, (((1,), (1,)), ((), ())), preferred_element_type=F32)


def store_cross_shifts(store, slab, row, width, columns):
    column = lax.broadcasted_iota(jnp.int32, (C, 128), 1) % columns
    for at in range(0, width, 128):
        part = slab[:, at : at + 128]
        back = jnp.where(column < columns - 1, pltpu.roll(part, 127, 1), 0.0)
        ahead = jnp.where(column > 0, pltpu.roll(part, 1, 1), 0.0)
        store[row : row + C, at : at + 128] = back.astype(BF)
        store[row + C : row + 2 * C, at : at + 128] = part.astype(BF)
        store[row + 2 * C : row + 3 * C, at : at + 128] = ahead.astype(BF)


def inline_sum(taps, columns):
    width = taps.shape[1]
    lane = lax.broadcasted_iota(jnp.int32, (C, width), 1)
    first = jnp.where(lane < width - columns, pltpu.roll(taps[:C], width - columns, 1), 0.0)
    last = jnp.where(lane >= columns, pltpu.roll(taps[2 * C :], columns, 1), 0.0)
    return taps[C : 2 * C] + first + last


def inline_shifts(saved, columns):
    wide = saved.astype(F32)
    width = wide.shape[1]
    lane = lax.broadcasted_iota(jnp.int32, (C, width), 1)
    first = jnp.where(lane >= columns, pltpu.roll(wide, columns, 1), 0.0)
    last = jnp.where(lane < width - columns, pltpu.roll(wide, width - columns, 1), 0.0)
    return jnp.concatenate([first.astype(BF), saved, last.astype(BF)], axis=0)


def write_edges(slabs, spread, pooled_ref, up_ref, down_ref):
    down_ref[:, :NF] = slabs[0]
    up_ref[:, :NF] = slabs[D - 1]
    sums = dot_nt(jnp.concatenate(slabs, axis=0), spread[...])
    for j in range(2):
        at = 2 * j * C
        pooled = (sums[at : at + C] + sums[at + C : at + 2 * C]).astype(BF)
        pooled_ref[:, j * NC : (j + 1) * NC] = pooled
        down_ref[:, NF + j * NC : NF + (j + 1) * NC] = pooled
        up_ref[:, NF + j * NC : NF + (j + 1) * NC] = pooled


def seed_kernel(weight_ref, cot_ref, label_ref, pre_ref, own_ref, up_ref, down_ref, spread_ref):
    spread_ref[...] = spread_matrix()
    slabs = []
    for d in range(D):
        label = label_ref[d : d + 1, :]
        weight = jnp.zeros(label.shape, F32)
        for k in range(3):
            weight = weight + jnp.where(label == k, weight_ref[k], 0.0)
        slabs.append((cot_ref[:, d * NF : (d + 1) * NF].astype(F32) * weight).astype(BF))
        own_ref[:, d * NF : (d + 1) * NF] = slabs[d]
    write_edges(slabs, spread_ref, own_ref.at[:, pl.ds(D * NF, 2 * NC)], up_ref, down_ref)
    down_ref[:, EDGE:] = pre_ref[:, :NF]
    up_ref[:, EDGE:] = pre_ref[:, (D - 1) * NF :]


FRONT_INS = 10
FRONT_SEMS = 8


def front_scratch():
    return [
        pltpu.VMEM((C, 6 * NC), BF), pltpu.VMEM((18 * C, NF), BF), pltpu.VMEM((18 * C, NC), BF),
        pltpu.VMEM((C, 6 * NF), BF), pltpu.VMEM((C, 6 * NC), BF), pltpu.VMEM((3 * C, 9 * C), BF),
        pltpu.VMEM((NC, NF), BF), pltpu.VMEM((C, OWN), BF), pltpu.SemaphoreType.DMA((FRONT_SEMS,)),
    ]


def front(ins, gz_ref, scratch):
    own_from, lo_ref, hi_ref, first_lo, first_hi, pre_from, coarse_pre_from, coarse_w_from, spread_from = ins
    coarse_gz, fine_store, coarse_store, pre, coarse_pre, coarse_w, spread, own, sems = scratch
    fine, coarse = pl.ds(0, D * NF), pl.ds(D * NF, 2 * NC)
    loads = [
        pltpu.make_async_copy(source, target, sems.at[at])
        for at, (source, target) in enumerate((
            (own_from.at[:, coarse], own.at[:, coarse]),
            (coarse_pre_from.at[:, pl.ds(0, 6 * NC)], coarse_pre),
            (coarse_w_from, coarse_w),
            (spread_from, spread),
            (first_lo.at[:, pl.ds(EDGE, NF)], pre.at[:, pl.ds(0, NF)]),
            (pre_from, pre.at[:, pl.ds(NF, D * NF)]),
            (first_hi.at[:, pl.ds(EDGE, NF)], pre.at[:, pl.ds(5 * NF, NF)]),
            (own_from.at[:, fine], own.at[:, fine]),
        ))
    ]
    for load in loads:
        load.start()
    for load in loads[:2]:
        load.wait()
    for j in range(6):
        source = (lo_ref, own, hi_ref)[j // 2]
        base = (NF, D * NF, NF)[j // 2] + (j % 2) * NC
        pooled = source[:, base : base + NC].astype(F32)
        mask = coarse_pre[:, j * NC : (j + 1) * NC].astype(F32) > 0
        gz = jnp.where(mask, pooled, 0.0)
        coarse_gz[:, j * NC : (j + 1) * NC] = gz.astype(BF)
        store_cross_shifts(coarse_store, gz, j * 3 * C, NC, HX)
    loads[2].wait()
    backs = []
    for j in range(4):
        taps = dot(coarse_w[...], coarse_store[j * 3 * C : (j + 3) * 3 * C, :])
        backs.append(inline_sum(taps, HX).astype(BF))
    loads[3].wait()
    spreads = dot(jnp.concatenate(backs, axis=0), spread[...])
    for load in loads[4:]:
        load.wait()
    for d in range(6):
        if d == 0:
            grad = lo_ref[:, :NF]
        elif d == 5:
            grad = hi_ref[:, :NF]
        else:
            grad = own[:, (d - 1) * NF : d * NF]
        j = (d + 1) // 2
        total = grad.astype(F32) + 0.125 * spreads[j * C : (j + 1) * C]
        gz = jnp.where(pre[:, d * NF : (d + 1) * NF].astype(F32) > 0, total, 0.0).astype(BF)
        gz_ref[:, d * NF : (d + 1) * NF] = gz
        store_cross_shifts(fine_store, gz.astype(F32), d * 3 * C, NF, XL)


def fine_slab(d, own, fine_w, fine_store):
    taps = dot(fine_w[...], fine_store[d * 3 * C : (d + 3) * 3 * C, :])
    grad = own[:, d * NF : (d + 1) * NF].astype(F32)
    return (grad + inline_sum(taps, XL)).astype(BF)


def turn_kernel(act_ref, *refs):
    ins, fine_w_from, outs = refs[: FRONT_INS - 1], refs[FRONT_INS - 1], refs[-19:]
    up_out, down_out, own_out, keep_gz, keep_coarse_gz, keep_grad = outs[:6]
    gz, fine_w, new, sems = outs[6:10]
    scratch = outs[10:]
    coarse_gz, fine_store, spread, own = scratch[0], scratch[1], scratch[6], scratch[7]

    @pl.when(act_ref[0] == 1)
    def _():
        weights = pltpu.make_async_copy(fine_w_from, fine_w, sems.at[0])
        weights.start()
        front(ins, gz, scratch)
        saves = [
            pltpu.make_async_copy(gz, keep_gz, sems.at[1]),
            pltpu.make_async_copy(coarse_gz, keep_coarse_gz, sems.at[2]),
        ]
        for save in saves:
            save.start()
        weights.wait()
        slabs = []
        for d in range(D):
            slabs.append(fine_slab(d, own, fine_w, fine_store))
            lanes = pl.ds(d * NF, NF)
            new[:, d * NF : (d + 1) * NF] = slabs[d]
            for at, target in ((3 + d, own_out), (3 + D + d, keep_grad)):
                saves.append(pltpu.make_async_copy(new.at[:, lanes], target.at[:, lanes], sems.at[at]))
                saves[-1].start()
        lanes = pl.ds(D * NF, 2 * NC)
        write_edges(slabs, spread, new.at[:, lanes], up_out, down_out)
        saves.append(pltpu.make_async_copy(new.at[:, lanes], own_out.at[:, lanes], sems.at[3 + 2 * D]))
        saves[-1].start()
        for save in saves:
            save.wait()


def last_kernel(act_ref, *refs):
    ins = refs[: FRONT_INS - 1]
    keep_gz, keep_coarse_gz, saved_from, out_ref, gz, saved, coarse_saved, sems = refs[FRONT_INS - 1 : FRONT_INS + 7]
    scratch = refs[FRONT_INS + 7 :]
    coarse_gz, fine_store, coarse_store = scratch[:3]
    loads = [
        pltpu.make_async_copy(saved_from, saved, sems.at[0]),
        pltpu.make_async_copy(ins[6].at[:, pl.ds(6 * NC, 2 * NC)], coarse_saved, sems.at[1]),
    ]

    for load in loads:
        load.start()

    @pl.when(act_ref[0] == 1)
    def _():
        front(ins, gz, scratch)

    @pl.when(act_ref[0] == 0)
    def _():
        kept = [
            pltpu.make_async_copy(keep_gz, gz, sems.at[2]),
            pltpu.make_async_copy(keep_coarse_gz, coarse_gz, sems.at[3]),
        ]
        for copy in kept:
            copy.start()
        for copy in kept:
            copy.wait()
        for j in range(6):
            store_cross_shifts(
                coarse_store, coarse_gz[:, j * NC : (j + 1) * NC].astype(F32), j * 3 * C, NC, HX
            )
        for d in range(6):
            store_cross_shifts(fine_store, gz[:, d * NF : (d + 1) * NF].astype(F32), d * 3 * C, NF, XL)

    for load in loads:
        load.wait()
    fine_total = None
    for d in range(D):
        moved = inline_shifts(saved[:, d * NF : (d + 1) * NF], XL)
        term = dot_nt(moved, fine_store[d * 3 * C : (d + 3) * 3 * C, :])
        fine_total = term if fine_total is None else fine_total + term
    total = None
    for j in range(2):
        moved = inline_shifts(coarse_saved[:, j * NC : (j + 1) * NC], HX)
        term = dot_nt(moved, coarse_store[(j + 1) * 3 * C : (j + 4) * 3 * C, :])
        total = term if total is None else total + term
    for inline_tap in range(3):
        for column in range(9):
            depth_tap, cross_tap = 2 - column // 3, column % 3
            tap = depth_tap * 9 + inline_tap * 3 + cross_tap
            rows, lanes = slice(inline_tap * C, (inline_tap + 1) * C), slice(column * C, (column + 1) * C)
            both = jnp.concatenate([fine_total[rows, lanes], total[rows, lanes]], axis=1)
            out_ref[tap * C : (tap + 1) * C, :] = both.astype(BF)


def grad_kernel(act_ref, gz, own, fine_w, kept, keep_grad, new, fine_store, sem):
    @pl.when(act_ref[0] == 1)
    def _():
        for d in range(6):
            store_cross_shifts(fine_store, gz[:, d * NF : (d + 1) * NF].astype(F32), d * 3 * C, NF, XL)
        for d in range(D):
            new[:, d * NF : (d + 1) * NF] = fine_slab(d, own, fine_w, fine_store)
        save = pltpu.make_async_copy(new, keep_grad, sem.at[0])
        save.start()
        save.wait()


VM = pl.BlockSpec(memory_space=pltpu.VMEM)
SM = pl.BlockSpec(memory_space=pltpu.SMEM)
HB = pl.BlockSpec(memory_space=pl.ANY)


def call(kernel, outs, ins, scratch, flops, args, keeps=(), aliases={}):
    moved = sum(a.size * a.dtype.itemsize for a in args)
    return pl.pallas_call(
        kernel,
        out_shape=[jax.ShapeDtypeStruct(shape, BF) for shape in tuple(outs) + tuple(keeps)],
        in_specs=ins,
        out_specs=[VM] * len(outs) + [HB] * len(keeps),
        scratch_shapes=scratch,
        input_output_aliases=aliases,
        compiler_params=pltpu.CompilerParams(vmem_limit_bytes=VMEM_LIMIT),
        cost_estimate=pl.CostEstimate(flops=flops, bytes_accessed=moved, transcendentals=0),
    )(*args)


def pack_rows(mask, saved):
    vols = lax.axis_size("vol")
    pairs = mask.reshape(C, vols, 2 * HX)
    padded = jnp.pad(pairs, ((0, 0), (1, 1), (0, 0)))
    parts = [padded[:, k : k + vols] for k in range(3)] + [saved.reshape(C, vols, 2 * HX)]
    return jnp.concatenate(parts, axis=2)


def depth_slices(packed):
    vols = lax.axis_size("vol")
    moved = lax.all_to_all(packed, "vol", split_axis=1, concat_axis=1, tiled=True)
    return jnp.transpose(moved.reshape(C, vols, 8, HX), (0, 2, 1, 3)).reshape(C, 8 * NC)


def hop(array, pairs):
    return lax.ppermute(array, ("segment", "vol"), pairs)


def reduce_all(partial):
    vols = lax.axis_size("vol")
    part = partial.reshape(vols, partial.shape[0] // vols, partial.shape[1])
    part = lax.all_to_all(part, "vol", 0, 0)
    part = part.astype(F32).sum(axis=0).astype(BF)
    part = jnp.broadcast_to(part[None], (vols,) + part.shape)
    part = lax.all_to_all(part, "vol", 0, 0)
    return part.reshape(partial.shape)


def on_device(
    cotangent, labels, class_weight, inputs, fine_pre, pooled, coarse_pre, fine_filters, coarse_filters
):
    segments = lax.axis_size("segment")
    vols = lax.axis_size("vol")
    position = lax.axis_index("segment")
    pre = fine_pre[0].reshape(C, D * NF)
    head_edge = EDGE + NF
    own, up, down, spread = call(
        seed_kernel, [(C, OWN), (C, head_edge), (C, head_edge), (NC, NF)], [SM, VM, VM, VM], [], 10**9,
        (class_weight, cotangent.reshape(C, D * NF), labels, pre),
    )
    first_lo = lax.ppermute(up, "vol", [(v, v + 1) for v in range(vols - 1)])
    first_hi = lax.ppermute(down, "vol", [(v + 1, v) for v in range(vols - 1)])
    packed, first_lo, first_hi = lax.optimization_barrier(
        (pack_rows(coarse_pre[0], pooled[0]), first_lo, first_hi)
    )
    coarse_both = depth_slices(packed)
    fine_w = filter_matrix(fine_filters[0])
    coarse_w = filter_matrix(coarse_filters[0])
    lo, hi = first_lo, first_hi
    keeps = ()
    for turn in range(segments - 1):
        s = segments - 1 - turn
        act = (position == s).astype(jnp.int32).reshape(1)
        up, down, own, *keeps = call(
            turn_kernel,
            [(C, EDGE), (C, EDGE)],
            [SM, HB, VM, VM] + [HB] * (7 + len(keeps)),
            [
                pltpu.VMEM((C, 6 * NF), BF), pltpu.VMEM((3 * C, 9 * C), BF), pltpu.VMEM((C, OWN), BF),
                pltpu.SemaphoreType.DMA((4 + 2 * D,)), *front_scratch(),
            ],
            4 * 10**9,
            (act, own, lo, hi, first_lo, first_hi, pre, coarse_both, coarse_w, spread, fine_w, *keeps),
            ((C, OWN), (C, 6 * NF), (C, 6 * NC), (C, D * NF)),
            {11 + k: 3 + k for k in range(len(keeps))},
        )
        base, to = s * vols, (s - 1) * vols
        lo = hop(up, [(base + v, to + v + 1) for v in range(vols - 1)])
        hi = hop(down, [(base + v + 1, to + v) for v in range(vols - 1)])
        own = hop(own, [(base + v, to + v) for v in range(vols)])
    act = (position == 0).astype(jnp.int32).reshape(1)
    keep_gz, keep_coarse_gz, keep_grad = keeps
    partial, gz = call(
        last_kernel,
        [(27 * C, 2 * C), (C, 6 * NF)],
        [SM, HB, VM, VM] + [HB] * 9,
        [
            pltpu.VMEM((C, D * NF), BF), pltpu.VMEM((C, 2 * NC), BF), pltpu.SemaphoreType.DMA((4,)),
            *front_scratch(),
        ],
        4 * 10**9,
        (
            act, own, lo, hi, first_lo, first_hi, pre, coarse_both, coarse_w, spread,
            keep_gz, keep_coarse_gz, inputs[0].reshape(C, D * NF),
        ),
    )
    (grad,) = call(
        grad_kernel, [], [SM, VM, VM, VM, HB],
        [pltpu.VMEM((C, D * NF), BF), pltpu.VMEM((18 * C, NF), BF), pltpu.SemaphoreType.DMA((1,))],
        2 * 10**9, (act, gz, own, fine_w, keep_grad), ((C, D * NF),), {4: 0},
    )
    total = reduce_all(partial)
    cells = D * vols * NF
    total = total.reshape(27, C, 2 * C).astype(F32)
    fine_total = total[:, :, :C] * (1.0 / math.sqrt(cells))
    coarse_total = total[:, :, C:] * (1.0 / math.sqrt(cells // 8))
    return grad.reshape(1, C, D, NF), fine_total[None], coarse_total[None]


def solution(mesh):
    return jax.shard_map(
        on_device,
        mesh=mesh,
        in_specs=(
            P(None, "vol", None),
            P("vol", None),
            P(),
            P("segment", None, "vol", None),
            P("segment", None, "vol", None),
            P("segment", None, "vol", None),
            P("segment", None, "vol", None),
            P("segment", None, None, None),
            P("segment", None, None, None),
        ),
        out_specs=(
            P("segment", None, "vol", None),
            P("segment", None, None, None),
            P("segment", None, None, None),
        ),
        check_vma=False,
    )
```

```python
import functools
import math

import jax
import jax.numpy as jnp
from jax import lax
from jax.experimental import pallas as pl
from jax.experimental.pallas import tpu as pltpu
from jax.sharding import PartitionSpec as P

XL = 16
HX = XL // 2
C = 64
D = 4
NF = 1024
NC = 256
EDGE = NF + 2 * NC
OWN = D * NF + 2 * NC
BF = jnp.bfloat16
F32 = jnp.float32
VMEM_LIMIT = 51500 * 1024


def spread_matrix():
    coarse = lax.broadcasted_iota(jnp.int32, (NC, NF), 0)
    fine = lax.broadcasted_iota(jnp.int32, (NC, NF), 1)
    owner = (fine // (2 * XL)) * HX + (fine % XL) // 2
    return jnp.where(coarse == owner, 1.0, 0.0).astype(BF)


def filter_matrix(weights):
    grid = weights.reshape(3, 3, 3, C, C)[::-1]
    return jnp.transpose(grid, (1, 3, 0, 2, 4)).reshape(3 * C, 9 * C)


def dot(a, b):
    return jnp.dot(a, b, preferred_element_type=F32)


def dot_nt(a, b):
    return lax.dot_general(a, b, (((1,), (1,)), ((), ())), preferred_element_type=F32)


def store_cross_shifts(store, slab, row, width, columns):
    column = lax.broadcasted_iota(jnp.int32, (C, 128), 1) % columns
    for at in range(0, width, 128):
        part = slab[:, at : at + 128]
        back = jnp.where(column < columns - 1, pltpu.roll(part, 127, 1), 0.0)
        ahead = jnp.where(column > 0, pltpu.roll(part, 1, 1), 0.0)
        store[row : row + C, at : at + 128] = back.astype(BF)
        store[row + C : row + 2 * C, at : at + 128] = part.astype(BF)
        store[row + 2 * C : row + 3 * C, at : at + 128] = ahead.astype(BF)


def inline_sum(taps, columns):
    width = taps.shape[1]
    lane = lax.broadcasted_iota(jnp.int32, (C, width), 1)
    first = jnp.where(lane < width - columns, pltpu.roll(taps[:C], width - columns, 1), 0.0)
    last = jnp.where(lane >= columns, pltpu.roll(taps[2 * C :], columns, 1), 0.0)
    return taps[C : 2 * C] + first + last


def inline_shifts(saved, columns):
    wide = saved.astype(F32)
    width = wide.shape[1]
    lane = lax.broadcasted_iota(jnp.int32, (C, width), 1)
    first = jnp.where(lane >= columns, pltpu.roll(wide, columns, 1), 0.0)
    last = jnp.where(lane < width - columns, pltpu.roll(wide, width - columns, 1), 0.0)
    return jnp.concatenate([first.astype(BF), saved, last.astype(BF)], axis=0)


def write_edges(slabs, spread, pooled_ref, up_ref, down_ref):
    down_ref[:, :NF] = slabs[0]
    up_ref[:, :NF] = slabs[D - 1]
    sums = dot_nt(jnp.concatenate(slabs, axis=0), spread[...])
    for j in range(2):
        at = 2 * j * C
        pooled = (sums[at : at + C] + sums[at + C : at + 2 * C]).astype(BF)
        pooled_ref[:, j * NC : (j + 1) * NC] = pooled
        down_ref[:, NF + j * NC : NF + (j + 1) * NC] = pooled
        up_ref[:, NF + j * NC : NF + (j + 1) * NC] = pooled


def seed_kernel(
    end, weight_ref, at_ref, cot_ref, label_ref, pre_ref, own_ref, even_ref, odd_ref, spread_ref
):
    spread_ref[...] = spread_matrix()
    slabs = []
    for d in range(D):
        label = label_ref[d : d + 1, :]
        weight = jnp.zeros(label.shape, F32)
        for k in range(3):
            weight = weight + jnp.where(label == k, weight_ref[k], 0.0)
        slabs.append((cot_ref[:, d * NF : (d + 1) * NF].astype(F32) * weight).astype(BF))
        own_ref[:, d * NF : (d + 1) * NF] = slabs[d]
    at = at_ref[0]
    pooled_ref = own_ref.at[:, pl.ds(D * NF, 2 * NC)]
    first, last = pre_ref[:, :NF], pre_ref[:, (D - 1) * NF :]

    @pl.when(at % 2 == 0)
    def _():
        write_edges(slabs, spread_ref, pooled_ref, even_ref, odd_ref)
        even_ref[:, EDGE:] = last
        odd_ref[:, EDGE:] = jnp.where(at == 0, 0.0, first.astype(F32)).astype(BF)

    @pl.when(at % 2 == 1)
    def _():
        write_edges(slabs, spread_ref, pooled_ref, odd_ref, even_ref)
        even_ref[:, EDGE:] = first
        odd_ref[:, EDGE:] = jnp.where(at == end, 0.0, last.astype(F32)).astype(BF)


FRONT_INS = 10
FRONT_SEMS = 8


def front_scratch():
    return [
        pltpu.VMEM((C, 6 * NC), BF), pltpu.VMEM((18 * C, NF), BF), pltpu.VMEM((18 * C, NC), BF),
        pltpu.VMEM((C, 6 * NF), BF), pltpu.VMEM((C, 6 * NC), BF), pltpu.VMEM((3 * C, 9 * C), BF),
        pltpu.VMEM((NC, NF), BF), pltpu.VMEM((C, OWN), BF), pltpu.SemaphoreType.DMA((FRONT_SEMS,)),
    ]


def front(ins, gz_ref, scratch):
    own_from, lo_ref, hi_ref, first_lo, first_hi, pre_from, coarse_pre_from, coarse_w_from, spread_from = ins
    coarse_gz, fine_store, coarse_store, pre, coarse_pre, coarse_w, spread, own, sems = scratch
    fine, coarse = pl.ds(0, D * NF), pl.ds(D * NF, 2 * NC)
    loads = [
        pltpu.make_async_copy(source, target, sems.at[at])
        for at, (source, target) in enumerate((
            (own_from.at[:, coarse], own.at[:, coarse]),
            (coarse_pre_from.at[:, pl.ds(0, 6 * NC)], coarse_pre),
            (coarse_w_from, coarse_w),
            (spread_from, spread),
            (first_lo.at[:, pl.ds(EDGE, NF)], pre.at[:, pl.ds(0, NF)]),
            (pre_from, pre.at[:, pl.ds(NF, D * NF)]),
            (first_hi.at[:, pl.ds(EDGE, NF)], pre.at[:, pl.ds(5 * NF, NF)]),
            (own_from.at[:, fine], own.at[:, fine]),
        ))
    ]
    for load in loads:
        load.start()
    for load in loads[:2]:
        load.wait()
    for j in range(6):
        source = (lo_ref, own, hi_ref)[j // 2]
        base = (NF, D * NF, NF)[j // 2] + (j % 2) * NC
        pooled = source[:, base : base + NC].astype(F32)
        mask = coarse_pre[:, j * NC : (j + 1) * NC].astype(F32) > 0
        gz = jnp.where(mask, pooled, 0.0)
        coarse_gz[:, j * NC : (j + 1) * NC] = gz.astype(BF)
        store_cross_shifts(coarse_store, gz, j * 3 * C, NC, HX)
    loads[2].wait()
    backs = []
    for j in range(4):
        taps = dot(coarse_w[...], coarse_store[j * 3 * C : (j + 3) * 3 * C, :])
        backs.append(inline_sum(taps, HX).astype(BF))
    loads[3].wait()
    spreads = dot(jnp.concatenate(backs, axis=0), spread[...])
    for load in loads[4:]:
        load.wait()
    for d in range(6):
        if d == 0:
            grad = lo_ref[:, :NF]
        elif d == 5:
            grad = hi_ref[:, :NF]
        else:
            grad = own[:, (d - 1) * NF : d * NF]
        j = (d + 1) // 2
        total = grad.astype(F32) + 0.125 * spreads[j * C : (j + 1) * C]
        gz = jnp.where(pre[:, d * NF : (d + 1) * NF].astype(F32) > 0, total, 0.0).astype(BF)
        gz_ref[:, d * NF : (d + 1) * NF] = gz
        store_cross_shifts(fine_store, gz.astype(F32), d * 3 * C, NF, XL)


def fine_slab(d, own, fine_w, fine_store):
    taps = dot(fine_w[...], fine_store[d * 3 * C : (d + 3) * 3 * C, :])
    grad = own[:, d * NF : (d + 1) * NF].astype(F32)
    return (grad + inline_sum(taps, XL)).astype(BF)


def turn_kernel(act_ref, *refs):
    ins, fine_w_from, outs = refs[: FRONT_INS - 1], refs[FRONT_INS - 1], refs[-18:]
    own_out, up_out, down_out, keep_gz, keep_coarse_gz, keep_grad = outs[:6]
    gz, fine_w, sems = outs[6:9]
    scratch = outs[9:]
    coarse_gz, fine_store, spread, own = scratch[0], scratch[1], scratch[6], scratch[7]

    @pl.when(act_ref[0] == 1)
    def _():
        weights = pltpu.make_async_copy(fine_w_from, fine_w, sems.at[0])
        weights.start()
        front(ins, gz, scratch)
        saves = [
            pltpu.make_async_copy(gz, keep_gz, sems.at[1]),
            pltpu.make_async_copy(coarse_gz, keep_coarse_gz, sems.at[2]),
        ]
        for save in saves:
            save.start()
        weights.wait()
        slabs = []
        for d in range(D):
            slabs.append(fine_slab(d, own, fine_w, fine_store))
            own_out[:, d * NF : (d + 1) * NF] = slabs[d]
        fine = pl.ds(0, D * NF)
        saves.append(pltpu.make_async_copy(own_out.at[:, fine], keep_grad, sems.at[3]))
        saves[-1].start()
        write_edges(slabs, spread, own_out.at[:, pl.ds(D * NF, 2 * NC)], up_out, down_out)
        for save in saves:
            save.wait()


def last_kernel(act_ref, *refs):
    ins = refs[: FRONT_INS - 1]
    keep_gz, keep_coarse_gz, saved_from, out_ref, gz, saved, coarse_saved, sems = refs[FRONT_INS - 1 : FRONT_INS + 7]
    scratch = refs[FRONT_INS + 7 :]
    coarse_gz, fine_store, coarse_store = scratch[:3]
    loads = [
        pltpu.make_async_copy(saved_from, saved, sems.at[0]),
        pltpu.make_async_copy(ins[6].at[:, pl.ds(6 * NC, 2 * NC)], coarse_saved, sems.at[1]),
    ]

    for load in loads:
        load.start()

    @pl.when(act_ref[0] == 1)
    def _():
        front(ins, gz, scratch)

    @pl.when(act_ref[0] == 0)
    def _():
        kept = [
            pltpu.make_async_copy(keep_gz, gz, sems.at[2]),
            pltpu.make_async_copy(keep_coarse_gz, coarse_gz, sems.at[3]),
        ]
        for copy in kept:
            copy.start()
        for copy in kept:
            copy.wait()
        for j in range(6):
            store_cross_shifts(
                coarse_store, coarse_gz[:, j * NC : (j + 1) * NC].astype(F32), j * 3 * C, NC, HX
            )
        for d in range(6):
            store_cross_shifts(fine_store, gz[:, d * NF : (d + 1) * NF].astype(F32), d * 3 * C, NF, XL)

    for load in loads:
        load.wait()
    fine_total = None
    for d in range(D):
        moved = inline_shifts(saved[:, d * NF : (d + 1) * NF], XL)
        term = dot_nt(moved, fine_store[d * 3 * C : (d + 3) * 3 * C, :])
        fine_total = term if fine_total is None else fine_total + term
    total = None
    for j in range(2):
        moved = inline_shifts(coarse_saved[:, j * NC : (j + 1) * NC], HX)
        term = dot_nt(moved, coarse_store[(j + 1) * 3 * C : (j + 4) * 3 * C, :])
        total = term if total is None else total + term
    for inline_tap in range(3):
        for column in range(9):
            depth_tap, cross_tap = 2 - column // 3, column % 3
            tap = depth_tap * 9 + inline_tap * 3 + cross_tap
            rows, lanes = slice(inline_tap * C, (inline_tap + 1) * C), slice(column * C, (column + 1) * C)
            both = jnp.concatenate([fine_total[rows, lanes], total[rows, lanes]], axis=1)
            out_ref[tap * C : (tap + 1) * C, :] = both.astype(BF)


def grad_kernel(act_ref, gz, own, fine_w, kept, keep_grad, new, fine_store, sem):
    @pl.when(act_ref[0] == 1)
    def _():
        for d in range(6):
            store_cross_shifts(fine_store, gz[:, d * NF : (d + 1) * NF].astype(F32), d * 3 * C, NF, XL)
        for d in range(D):
            new[:, d * NF : (d + 1) * NF] = fine_slab(d, own, fine_w, fine_store)
        save = pltpu.make_async_copy(new, keep_grad, sem.at[0])
        save.start()
        save.wait()


VM = pl.BlockSpec(memory_space=pltpu.VMEM)
SM = pl.BlockSpec(memory_space=pltpu.SMEM)
HB = pl.BlockSpec(memory_space=pl.ANY)


def call(kernel, outs, ins, scratch, flops, args, keeps=(), aliases={}):
    moved = sum(a.size * a.dtype.itemsize for a in args)
    return pl.pallas_call(
        kernel,
        out_shape=[jax.ShapeDtypeStruct(shape, BF) for shape in tuple(outs) + tuple(keeps)],
        in_specs=ins,
        out_specs=[VM] * len(outs) + [HB] * len(keeps),
        scratch_shapes=scratch,
        input_output_aliases=aliases,
        compiler_params=pltpu.CompilerParams(vmem_limit_bytes=VMEM_LIMIT),
        cost_estimate=pl.CostEstimate(flops=flops, bytes_accessed=moved, transcendentals=0),
    )(*args)


def pack_rows(mask, saved):
    vols = lax.axis_size("vol")
    pairs = mask.reshape(C, vols, 2 * HX)
    padded = jnp.pad(pairs, ((0, 0), (1, 1), (0, 0)))
    parts = [padded[:, k : k + vols] for k in range(3)] + [saved.reshape(C, vols, 2 * HX)]
    return jnp.concatenate(parts, axis=2)


def depth_slices(packed):
    vols = lax.axis_size("vol")
    moved = lax.all_to_all(packed, "vol", split_axis=1, concat_axis=1, tiled=True)
    return jnp.transpose(moved.reshape(C, vols, 8, HX), (0, 2, 1, 3)).reshape(C, 8 * NC)


def hop(array, pairs):
    return lax.ppermute(array, ("segment", "vol"), pairs)


def reduce_all(partial):
    vols = lax.axis_size("vol")
    part = partial.reshape(vols, partial.shape[0] // vols, partial.shape[1])
    part = lax.all_to_all(part, "vol", 0, 0)
    part = part.astype(F32).sum(axis=0).astype(BF)
    part = jnp.broadcast_to(part[None], (vols,) + part.shape)
    part = lax.all_to_all(part, "vol", 0, 0)
    return part.reshape(partial.shape)


def on_device(
    cotangent, labels, class_weight, inputs, fine_pre, pooled, coarse_pre, fine_filters, coarse_filters
):
    segments = lax.axis_size("segment")
    vols = lax.axis_size("vol")
    position = lax.axis_index("segment")
    pre = fine_pre[0].reshape(C, D * NF)
    head_edge = EDGE + NF
    at = lax.axis_index("vol")
    own, even, odd, spread = call(
        functools.partial(seed_kernel, vols - 1),
        [(C, OWN), (C, head_edge), (C, head_edge), (NC, NF)], [SM, SM, VM, VM, VM], [], 10**9,
        (class_weight, at.astype(jnp.int32).reshape(1), cotangent.reshape(C, D * NF), labels, pre),
    )
    odd = lax.ppermute(odd, "vol", [(v, (v + (1 if v % 2 else -1)) % vols) for v in range(vols)])
    even = lax.ppermute(even, "vol", [(v, v ^ 1) for v in range(vols)])
    first_lo = jnp.where(at % 2 == 0, odd, even)
    first_hi = jnp.where(at % 2 == 0, even, odd)
    coarse_both = depth_slices(pack_rows(coarse_pre[0], pooled[0]))
    fine_w = filter_matrix(fine_filters[0])
    coarse_w = filter_matrix(coarse_filters[0])
    lo, hi = first_lo, first_hi
    keeps = ()
    for turn in range(segments - 1):
        s = segments - 1 - turn
        act = (position == s).astype(jnp.int32).reshape(1)
        own, up, down, *keeps = call(
            turn_kernel,
            [(C, OWN), (C, EDGE), (C, EDGE)],
            [SM, HB, VM, VM] + [HB] * (7 + len(keeps)),
            [
                pltpu.VMEM((C, 6 * NF), BF), pltpu.VMEM((3 * C, 9 * C), BF), pltpu.SemaphoreType.DMA((4,)),
                *front_scratch(),
            ],
            4 * 10**9,
            (act, own, lo, hi, first_lo, first_hi, pre, coarse_both, coarse_w, spread, fine_w, *keeps),
            ((C, 6 * NF), (C, 6 * NC), (C, D * NF)),
            {11 + k: 3 + k for k in range(len(keeps))},
        )
        base, to = s * vols, (s - 1) * vols
        lo = hop(up, [(base + v, to + v + 1) for v in range(vols - 1)])
        hi = hop(down, [(base + v + 1, to + v) for v in range(vols - 1)])
        own = hop(own, [(base + v, to + v) for v in range(vols)])
    act = (position == 0).astype(jnp.int32).reshape(1)
    keep_gz, keep_coarse_gz, keep_grad = keeps
    partial, gz = call(
        last_kernel,
        [(27 * C, 2 * C), (C, 6 * NF)],
        [SM, HB, VM, VM] + [HB] * 9,
        [
            pltpu.VMEM((C, D * NF), BF), pltpu.VMEM((C, 2 * NC), BF), pltpu.SemaphoreType.DMA((4,)),
            *front_scratch(),
        ],
        4 * 10**9,
        (
            act, own, lo, hi, first_lo, first_hi, pre, coarse_both, coarse_w, spread,
            keep_gz, keep_coarse_gz, inputs[0].reshape(C, D * NF),
        ),
    )
    (grad,) = call(
        grad_kernel, [], [SM, VM, VM, VM, HB],
        [pltpu.VMEM((C, D * NF), BF), pltpu.VMEM((18 * C, NF), BF), pltpu.SemaphoreType.DMA((1,))],
        2 * 10**9, (act, gz, own, fine_w, keep_grad), ((C, D * NF),), {4: 0},
    )
    total = reduce_all(partial)
    cells = D * vols * NF
    total = total.reshape(27, C, 2 * C).astype(F32)
    fine_total = total[:, :, :C] * (1.0 / math.sqrt(cells))
    coarse_total = total[:, :, C:] * (1.0 / math.sqrt(cells // 8))
    return grad.reshape(1, C, D, NF), fine_total[None], coarse_total[None]


def solution(mesh):
    return jax.shard_map(
        on_device,
        mesh=mesh,
        in_specs=(
            P(None, "vol", None),
            P("vol", None),
            P(),
            P("segment", None, "vol", None),
            P("segment", None, "vol", None),
            P("segment", None, "vol", None),
            P("segment", None, "vol", None),
            P("segment", None, None, None),
            P("segment", None, None, None),
        ),
        out_specs=(
            P("segment", None, "vol", None),
            P("segment", None, None, None),
            P("segment", None, None, None),
        ),
        check_vma=False,
    )
```

```python
import functools
import math

import jax
import jax.numpy as jnp
from jax import lax
from jax.experimental import pallas as pl
from jax.experimental.pallas import tpu as pltpu
from jax.sharding import PartitionSpec as P

XL = 16
HX = XL // 2
C = 64
D = 4
NF = 1024
NC = 256
EDGE = NF + 2 * NC
OWN = D * NF + 2 * NC
BF = jnp.bfloat16
F32 = jnp.float32
SEED_VMEM = 58000 * 1024
TURN_VMEM = 53000 * 1024
LAST_VMEM = 53000 * 1024
GRAD_VMEM = 53000 * 1024


def spread_matrix():
    coarse = lax.broadcasted_iota(jnp.int32, (NC, NF), 0)
    fine = lax.broadcasted_iota(jnp.int32, (NC, NF), 1)
    owner = (fine // (2 * XL)) * HX + (fine % XL) // 2
    return jnp.where(coarse == owner, 1.0, 0.0).astype(BF)


def filter_matrix(weights):
    grid = weights.reshape(3, 3, 3, C, C)[::-1]
    return jnp.transpose(grid, (1, 3, 0, 2, 4)).reshape(3 * C, 9 * C)


def dot(a, b):
    return jnp.dot(a, b, preferred_element_type=F32)


def dot_nt(a, b):
    return lax.dot_general(a, b, (((1,), (1,)), ((), ())), preferred_element_type=F32)


def store_cross_shifts(store, slab, row, width, columns):
    column = lax.broadcasted_iota(jnp.int32, (C, 128), 1) % columns
    for at in range(0, width, 128):
        part = slab[:, at : at + 128]
        back = jnp.where(column < columns - 1, pltpu.roll(part, 127, 1), 0.0)
        ahead = jnp.where(column > 0, pltpu.roll(part, 1, 1), 0.0)
        store[row : row + C, at : at + 128] = back.astype(BF)
        store[row + C : row + 2 * C, at : at + 128] = part.astype(BF)
        store[row + 2 * C : row + 3 * C, at : at + 128] = ahead.astype(BF)


def inline_sum(taps, columns):
    width = taps.shape[1]
    lane = lax.broadcasted_iota(jnp.int32, (C, width), 1)
    first = jnp.where(lane < width - columns, pltpu.roll(taps[:C], width - columns, 1), 0.0)
    last = jnp.where(lane >= columns, pltpu.roll(taps[2 * C :], columns, 1), 0.0)
    return taps[C : 2 * C] + first + last


def inline_shifts(saved, columns):
    wide = saved.astype(F32)
    width = wide.shape[1]
    lane = lax.broadcasted_iota(jnp.int32, (C, width), 1)
    first = jnp.where(lane >= columns, pltpu.roll(wide, columns, 1), 0.0)
    last = jnp.where(lane < width - columns, pltpu.roll(wide, width - columns, 1), 0.0)
    return jnp.concatenate([first.astype(BF), saved, last.astype(BF)], axis=0)


def write_edges(slabs, spread, pooled_ref, up_ref, down_ref):
    down_ref[:, :NF] = slabs[0]
    up_ref[:, :NF] = slabs[D - 1]
    sums = dot_nt(jnp.concatenate(slabs, axis=0), spread[...])
    for j in range(2):
        at = 2 * j * C
        pooled = (sums[at : at + C] + sums[at + C : at + 2 * C]).astype(BF)
        pooled_ref[:, j * NC : (j + 1) * NC] = pooled
        down_ref[:, NF + j * NC : NF + (j + 1) * NC] = pooled
        up_ref[:, NF + j * NC : NF + (j + 1) * NC] = pooled


def seed_kernel(
    end, weight_ref, at_ref, cot_ref, label_ref, pre_ref, own_ref, even_ref, odd_ref, spread_ref
):
    spread_ref[...] = spread_matrix()
    slabs = []
    for d in range(D):
        label = label_ref[d : d + 1, :]
        weight = jnp.zeros(label.shape, F32)
        for k in range(3):
            weight = weight + jnp.where(label == k, weight_ref[k], 0.0)
        slabs.append((cot_ref[:, d * NF : (d + 1) * NF].astype(F32) * weight).astype(BF))
        own_ref[:, d * NF : (d + 1) * NF] = slabs[d]
    at = at_ref[0]
    pooled_ref = own_ref.at[:, pl.ds(D * NF, 2 * NC)]
    first, last = pre_ref[:, :NF], pre_ref[:, (D - 1) * NF :]

    @pl.when(at % 2 == 0)
    def _():
        write_edges(slabs, spread_ref, pooled_ref, even_ref, odd_ref)
        even_ref[:, EDGE:] = last
        odd_ref[:, EDGE:] = jnp.where(at == 0, 0.0, first.astype(F32)).astype(BF)

    @pl.when(at % 2 == 1)
    def _():
        write_edges(slabs, spread_ref, pooled_ref, odd_ref, even_ref)
        even_ref[:, EDGE:] = first
        odd_ref[:, EDGE:] = jnp.where(at == end, 0.0, last.astype(F32)).astype(BF)


FRONT_INS = 10
FRONT_SEMS = 8


def front_scratch():
    return [
        pltpu.VMEM((C, 6 * NC), BF), pltpu.VMEM((18 * C, NF), BF), pltpu.VMEM((18 * C, NC), BF),
        pltpu.VMEM((C, 6 * NF), BF), pltpu.VMEM((C, 6 * NC), BF), pltpu.VMEM((3 * C, 9 * C), BF),
        pltpu.VMEM((NC, NF), BF), pltpu.VMEM((C, OWN), BF), pltpu.SemaphoreType.DMA((FRONT_SEMS,)),
    ]


def front(ins, gz_ref, scratch):
    own_from, lo_ref, hi_ref, first_lo, first_hi, pre_from, coarse_pre_from, coarse_w_from, spread_from = ins
    coarse_gz, fine_store, coarse_store, pre, coarse_pre, coarse_w, spread, own, sems = scratch
    fine, coarse = pl.ds(0, D * NF), pl.ds(D * NF, 2 * NC)
    loads = [
        pltpu.make_async_copy(source, target, sems.at[at])
        for at, (source, target) in enumerate((
            (own_from.at[:, coarse], own.at[:, coarse]),
            (coarse_pre_from.at[:, pl.ds(0, 6 * NC)], coarse_pre),
            (coarse_w_from, coarse_w),
            (spread_from, spread),
            (first_lo.at[:, pl.ds(EDGE, NF)], pre.at[:, pl.ds(0, NF)]),
            (pre_from, pre.at[:, pl.ds(NF, D * NF)]),
            (first_hi.at[:, pl.ds(EDGE, NF)], pre.at[:, pl.ds(5 * NF, NF)]),
            (own_from.at[:, fine], own.at[:, fine]),
        ))
    ]
    for load in loads:
        load.start()
    for load in loads[:2]:
        load.wait()
    for j in range(6):
        source = (lo_ref, own, hi_ref)[j // 2]
        base = (NF, D * NF, NF)[j // 2] + (j % 2) * NC
        pooled = source[:, base : base + NC].astype(F32)
        mask = coarse_pre[:, j * NC : (j + 1) * NC].astype(F32) > 0
        gz = jnp.where(mask, pooled, 0.0)
        coarse_gz[:, j * NC : (j + 1) * NC] = gz.astype(BF)
        store_cross_shifts(coarse_store, gz, j * 3 * C, NC, HX)
    loads[2].wait()
    backs = []
    for j in range(4):
        taps = dot(coarse_w[...], coarse_store[j * 3 * C : (j + 3) * 3 * C, :])
        backs.append(inline_sum(taps, HX).astype(BF))
    loads[3].wait()
    spreads = dot(jnp.concatenate(backs, axis=0), spread[...])
    for load in loads[4:]:
        load.wait()
    for d in range(6):
        if d == 0:
            grad = lo_ref[:, :NF]
        elif d == 5:
            grad = hi_ref[:, :NF]
        else:
            grad = own[:, (d - 1) * NF : d * NF]
        j = (d + 1) // 2
        total = grad.astype(F32) + 0.125 * spreads[j * C : (j + 1) * C]
        gz = jnp.where(pre[:, d * NF : (d + 1) * NF].astype(F32) > 0, total, 0.0).astype(BF)
        gz_ref[:, d * NF : (d + 1) * NF] = gz
        store_cross_shifts(fine_store, gz.astype(F32), d * 3 * C, NF, XL)


def fine_slab(d, own, fine_w, fine_store):
    taps = dot(fine_w[...], fine_store[d * 3 * C : (d + 3) * 3 * C, :])
    grad = own[:, d * NF : (d + 1) * NF].astype(F32)
    return (grad + inline_sum(taps, XL)).astype(BF)


def turn_kernel(act_ref, *refs):
    ins, fine_w_from, outs = refs[: FRONT_INS - 1], refs[FRONT_INS - 1], refs[-18:]
    own_out, up_out, down_out, keep_gz, keep_coarse_gz, keep_grad = outs[:6]
    gz, fine_w, sems = outs[6:9]
    scratch = outs[9:]
    coarse_gz, fine_store, spread, own = scratch[0], scratch[1], scratch[6], scratch[7]

    @pl.when(act_ref[0] == 1)
    def _():
        weights = pltpu.make_async_copy(fine_w_from, fine_w, sems.at[0])
        weights.start()
        front(ins, gz, scratch)
        saves = [
            pltpu.make_async_copy(gz, keep_gz, sems.at[1]),
            pltpu.make_async_copy(coarse_gz, keep_coarse_gz, sems.at[2]),
        ]
        for save in saves:
            save.start()
        weights.wait()
        slabs = []
        for d in range(D):
            slabs.append(fine_slab(d, own, fine_w, fine_store))
            own_out[:, d * NF : (d + 1) * NF] = slabs[d]
        fine = pl.ds(0, D * NF)
        saves.append(pltpu.make_async_copy(own_out.at[:, fine], keep_grad, sems.at[3]))
        saves[-1].start()
        write_edges(slabs, spread, own_out.at[:, pl.ds(D * NF, 2 * NC)], up_out, down_out)
        for save in saves:
            save.wait()


def last_kernel(act_ref, *refs):
    ins = refs[: FRONT_INS - 1]
    keep_gz, keep_coarse_gz, saved_from, out_ref, gz, saved, coarse_saved, sems = refs[FRONT_INS - 1 : FRONT_INS + 7]
    scratch = refs[FRONT_INS + 7 :]
    coarse_gz, fine_store, coarse_store = scratch[:3]
    loads = [
        pltpu.make_async_copy(saved_from, saved, sems.at[0]),
        pltpu.make_async_copy(ins[6].at[:, pl.ds(6 * NC, 2 * NC)], coarse_saved, sems.at[1]),
    ]

    for load in loads:
        load.start()

    @pl.when(act_ref[0] == 1)
    def _():
        front(ins, gz, scratch)

    @pl.when(act_ref[0] == 0)
    def _():
        kept = [
            pltpu.make_async_copy(keep_gz, gz, sems.at[2]),
            pltpu.make_async_copy(keep_coarse_gz, coarse_gz, sems.at[3]),
        ]
        for copy in kept:
            copy.start()
        for copy in kept:
            copy.wait()
        for j in range(6):
            store_cross_shifts(
                coarse_store, coarse_gz[:, j * NC : (j + 1) * NC].astype(F32), j * 3 * C, NC, HX
            )
        for d in range(6):
            store_cross_shifts(fine_store, gz[:, d * NF : (d + 1) * NF].astype(F32), d * 3 * C, NF, XL)

    for load in loads:
        load.wait()
    fine_total = None
    for d in range(D):
        moved = inline_shifts(saved[:, d * NF : (d + 1) * NF], XL)
        term = dot_nt(moved, fine_store[d * 3 * C : (d + 3) * 3 * C, :])
        fine_total = term if fine_total is None else fine_total + term
    total = None
    for j in range(2):
        moved = inline_shifts(coarse_saved[:, j * NC : (j + 1) * NC], HX)
        term = dot_nt(moved, coarse_store[(j + 1) * 3 * C : (j + 4) * 3 * C, :])
        total = term if total is None else total + term
    out_ref[27 * C :, :] = jnp.zeros((C, 2 * C), BF)
    for inline_tap in range(3):
        for column in range(9):
            depth_tap, cross_tap = 2 - column // 3, column % 3
            tap = depth_tap * 9 + inline_tap * 3 + cross_tap
            rows, lanes = slice(inline_tap * C, (inline_tap + 1) * C), slice(column * C, (column + 1) * C)
            both = jnp.concatenate([fine_total[rows, lanes], total[rows, lanes]], axis=1)
            out_ref[tap * C : (tap + 1) * C, :] = both.astype(BF)


def grad_kernel(act_ref, gz, own, fine_w, kept, keep_grad, new, fine_store, sem):
    @pl.when(act_ref[0] == 1)
    def _():
        for d in range(6):
            store_cross_shifts(fine_store, gz[:, d * NF : (d + 1) * NF].astype(F32), d * 3 * C, NF, XL)
        for d in range(D):
            new[:, d * NF : (d + 1) * NF] = fine_slab(d, own, fine_w, fine_store)
        save = pltpu.make_async_copy(new, keep_grad, sem.at[0])
        save.start()
        save.wait()


VM = pl.BlockSpec(memory_space=pltpu.VMEM)
SM = pl.BlockSpec(memory_space=pltpu.SMEM)
HB = pl.BlockSpec(memory_space=pl.ANY)


def call(kernel, vmem, outs, ins, scratch, flops, args, keeps=(), aliases={}):
    moved = sum(a.size * a.dtype.itemsize for a in args)
    return pl.pallas_call(
        kernel,
        out_shape=[jax.ShapeDtypeStruct(shape, BF) for shape in tuple(outs) + tuple(keeps)],
        in_specs=ins,
        out_specs=[VM] * len(outs) + [HB] * len(keeps),
        scratch_shapes=scratch,
        input_output_aliases=aliases,
        compiler_params=pltpu.CompilerParams(vmem_limit_bytes=vmem),
        cost_estimate=pl.CostEstimate(flops=flops, bytes_accessed=moved, transcendentals=0),
    )(*args)


def pack_rows(mask, saved):
    vols = lax.axis_size("vol")
    pairs = mask.reshape(C, vols, 2 * HX)
    padded = jnp.pad(pairs, ((0, 0), (1, 1), (0, 0)))
    parts = [padded[:, k : k + vols] for k in range(3)] + [saved.reshape(C, vols, 2 * HX)]
    return jnp.concatenate(parts, axis=2)


def depth_slices(packed):
    vols = lax.axis_size("vol")
    moved = lax.all_to_all(packed, "vol", split_axis=1, concat_axis=1, tiled=True)
    return jnp.transpose(moved.reshape(C, vols, 8, HX), (0, 2, 1, 3)).reshape(C, 8 * NC)


def hop(array, pairs):
    return lax.ppermute(array, ("segment", "vol"), pairs)


def reduce_all(partial):
    vols = lax.axis_size("vol")
    part = partial.reshape(vols, partial.shape[0] // vols, partial.shape[1])
    part = lax.all_to_all(part, "vol", 0, 0)
    part = part.astype(F32).sum(axis=0).astype(BF)
    part = jnp.broadcast_to(part[None], (vols,) + part.shape)
    part = lax.all_to_all(part, "vol", 0, 0)
    return part.reshape(partial.shape)


def on_device(
    cotangent, labels, class_weight, inputs, fine_pre, pooled, coarse_pre, fine_filters, coarse_filters
):
    segments = lax.axis_size("segment")
    vols = lax.axis_size("vol")
    position = lax.axis_index("segment")
    pre = fine_pre[0].reshape(C, D * NF)
    head_edge = EDGE + NF
    at = lax.axis_index("vol")
    own, even, odd, spread = call(
        functools.partial(seed_kernel, vols - 1), SEED_VMEM,
        [(C, OWN), (C, head_edge), (C, head_edge), (NC, NF)], [SM, SM, VM, VM, VM], [], 10**9,
        (class_weight, at.astype(jnp.int32).reshape(1), cotangent.reshape(C, D * NF), labels, pre),
    )
    odd = lax.ppermute(odd, "vol", [(v, (v + (1 if v % 2 else -1)) % vols) for v in range(vols)])
    even = lax.ppermute(even, "vol", [(v, v ^ 1) for v in range(vols)])
    first_lo = jnp.where(at % 2 == 0, odd, even)
    first_hi = jnp.where(at % 2 == 0, even, odd)
    coarse_both = depth_slices(pack_rows(coarse_pre[0], pooled[0]))
    coarse_both, saved = lax.optimization_barrier((coarse_both, inputs[0].reshape(C, D * NF)))
    fine_w = filter_matrix(fine_filters[0])
    coarse_w = filter_matrix(coarse_filters[0])
    lo, hi = first_lo, first_hi
    keeps = ()
    for turn in range(segments - 1):
        s = segments - 1 - turn
        act = (position == s).astype(jnp.int32).reshape(1)
        own, up, down, *keeps = call(
            turn_kernel, TURN_VMEM,
            [(C, OWN), (C, EDGE), (C, EDGE)],
            [SM, HB, VM, VM] + [HB] * (7 + len(keeps)),
            [
                pltpu.VMEM((C, 6 * NF), BF), pltpu.VMEM((3 * C, 9 * C), BF), pltpu.SemaphoreType.DMA((4,)),
                *front_scratch(),
            ],
            4 * 10**9,
            (act, own, lo, hi, first_lo, first_hi, pre, coarse_both, coarse_w, spread, fine_w, *keeps),
            ((C, 6 * NF), (C, 6 * NC), (C, D * NF)),
            {11 + k: 3 + k for k in range(len(keeps))},
        )
        base, to = s * vols, (s - 1) * vols
        lo = hop(up, [(base + v, to + v + 1) for v in range(vols - 1)])
        hi = hop(down, [(base + v + 1, to + v) for v in range(vols - 1)])
        own = hop(own, [(base + v, to + v) for v in range(vols)])
    act = (position == 0).astype(jnp.int32).reshape(1)
    keep_gz, keep_coarse_gz, keep_grad = keeps
    partial, gz = call(
        last_kernel, LAST_VMEM,
        [(28 * C, 2 * C), (C, 6 * NF)],
        [SM, HB, VM, VM] + [HB] * 9,
        [
            pltpu.VMEM((C, D * NF), BF), pltpu.VMEM((C, 2 * NC), BF), pltpu.SemaphoreType.DMA((4,)),
            *front_scratch(),
        ],
        4 * 10**9,
        (
            act, own, lo, hi, first_lo, first_hi, pre, coarse_both, coarse_w, spread,
            keep_gz, keep_coarse_gz, saved,
        ),
    )
    (grad,) = call(
        grad_kernel, GRAD_VMEM, [], [SM, VM, VM, VM, HB],
        [pltpu.VMEM((C, D * NF), BF), pltpu.VMEM((18 * C, NF), BF), pltpu.SemaphoreType.DMA((1,))],
        2 * 10**9, (act, gz, own, fine_w, keep_grad), ((C, D * NF),), {4: 0},
    )
    total = reduce_all(partial)
    cells = D * vols * NF
    total = total[: 27 * C].reshape(27, C, 2 * C).astype(F32)
    fine_total = total[:, :, :C] * (1.0 / math.sqrt(cells))
    coarse_total = total[:, :, C:] * (1.0 / math.sqrt(cells // 8))
    return grad.reshape(1, C, D, NF), fine_total[None], coarse_total[None]


def solution(mesh):
    return jax.shard_map(
        on_device,
        mesh=mesh,
        in_specs=(
            P(None, "vol", None),
            P("vol", None),
            P(),
            P("segment", None, "vol", None),
            P("segment", None, "vol", None),
            P("segment", None, "vol", None),
            P("segment", None, "vol", None),
            P("segment", None, None, None),
            P("segment", None, None, None),
        ),
        out_specs=(
            P("segment", None, "vol", None),
            P("segment", None, None, None),
            P("segment", None, None, None),
        ),
        check_vma=False,
    )
```

```python
import functools
import math

import jax
import jax.numpy as jnp
from jax import lax
from jax.experimental import pallas as pl
from jax.experimental.pallas import tpu as pltpu
from jax.sharding import PartitionSpec as P

XL = 16
HX = XL // 2
C = 64
D = 4
NF = 1024
NC = 256
EDGE = NF + 2 * NC
OWN = D * NF + 2 * NC
BF = jnp.bfloat16
F32 = jnp.float32
SEED_VMEM = 58000 * 1024
TURN_VMEM = 53000 * 1024
LAST_VMEM = 53000 * 1024
GRAD_VMEM = 53000 * 1024


def spread_matrix():
    coarse = lax.broadcasted_iota(jnp.int32, (NC, NF), 0)
    fine = lax.broadcasted_iota(jnp.int32, (NC, NF), 1)
    owner = (fine // (2 * XL)) * HX + (fine % XL) // 2
    return jnp.where(coarse == owner, 1.0, 0.0).astype(BF)


def filter_matrix(weights):
    grid = weights.reshape(3, 3, 3, C, C)[::-1]
    return jnp.transpose(grid, (1, 3, 0, 2, 4)).reshape(3 * C, 9 * C)


def dot(a, b):
    return jnp.dot(a, b, preferred_element_type=F32)


def dot_nt(a, b):
    return lax.dot_general(a, b, (((1,), (1,)), ((), ())), preferred_element_type=F32)


def store_cross_shifts(store, slab, row, width, columns):
    column = lax.broadcasted_iota(jnp.int32, (C, 128), 1) % columns
    for at in range(0, width, 128):
        part = slab[:, at : at + 128]
        back = jnp.where(column < columns - 1, pltpu.roll(part, 127, 1), 0.0)
        ahead = jnp.where(column > 0, pltpu.roll(part, 1, 1), 0.0)
        store[row : row + C, at : at + 128] = back.astype(BF)
        store[row + C : row + 2 * C, at : at + 128] = part.astype(BF)
        store[row + 2 * C : row + 3 * C, at : at + 128] = ahead.astype(BF)


def inline_sum(taps, columns):
    width = taps.shape[1]
    lane = lax.broadcasted_iota(jnp.int32, (C, width), 1)
    first = jnp.where(lane < width - columns, pltpu.roll(taps[:C], width - columns, 1), 0.0)
    last = jnp.where(lane >= columns, pltpu.roll(taps[2 * C :], columns, 1), 0.0)
    return taps[C : 2 * C] + first + last


def inline_shifts(saved, columns):
    wide = saved.astype(F32)
    width = wide.shape[1]
    lane = lax.broadcasted_iota(jnp.int32, (C, width), 1)
    first = jnp.where(lane >= columns, pltpu.roll(wide, columns, 1), 0.0)
    last = jnp.where(lane < width - columns, pltpu.roll(wide, width - columns, 1), 0.0)
    return jnp.concatenate([first.astype(BF), saved, last.astype(BF)], axis=0)


def write_edges(slabs, spread, pooled_ref, up_ref, down_ref):
    down_ref[:, :NF] = slabs[0]
    up_ref[:, :NF] = slabs[D - 1]
    sums = dot_nt(jnp.concatenate(slabs, axis=0), spread[...])
    for j in range(2):
        at = 2 * j * C
        pooled = (sums[at : at + C] + sums[at + C : at + 2 * C]).astype(BF)
        pooled_ref[:, j * NC : (j + 1) * NC] = pooled
        down_ref[:, NF + j * NC : NF + (j + 1) * NC] = pooled
        up_ref[:, NF + j * NC : NF + (j + 1) * NC] = pooled


def seed_kernel(
    end, weight_ref, at_ref, cot_ref, label_ref, pre_ref, own_ref, even_ref, odd_ref, spread_ref
):
    spread_ref[...] = spread_matrix()
    slabs = []
    for d in range(D):
        label = label_ref[d : d + 1, :]
        weight = jnp.zeros(label.shape, F32)
        for k in range(3):
            weight = weight + jnp.where(label == k, weight_ref[k], 0.0)
        slabs.append((cot_ref[:, d * NF : (d + 1) * NF].astype(F32) * weight).astype(BF))
        own_ref[:, d * NF : (d + 1) * NF] = slabs[d]
    at = at_ref[0]
    pooled_ref = own_ref.at[:, pl.ds(D * NF, 2 * NC)]
    first, last = pre_ref[:, :NF], pre_ref[:, (D - 1) * NF :]

    @pl.when(at % 2 == 0)
    def _():
        write_edges(slabs, spread_ref, pooled_ref, even_ref, odd_ref)
        even_ref[:, EDGE:] = last
        odd_ref[:, EDGE:] = jnp.where(at == 0, 0.0, first.astype(F32)).astype(BF)

    @pl.when(at % 2 == 1)
    def _():
        write_edges(slabs, spread_ref, pooled_ref, odd_ref, even_ref)
        even_ref[:, EDGE:] = first
        odd_ref[:, EDGE:] = jnp.where(at == end, 0.0, last.astype(F32)).astype(BF)


FRONT_INS = 9
FRONT_SEMS = 7


def front_scratch():
    return [
        pltpu.VMEM((C, 6 * NC), BF), pltpu.VMEM((18 * C, NF), BF), pltpu.VMEM((18 * C, NC), BF),
        pltpu.VMEM((C, 6 * NF), BF), pltpu.VMEM((C, 6 * NC), BF), pltpu.VMEM((3 * C, 9 * C), BF),
        pltpu.VMEM((NC, NF), BF), pltpu.VMEM((C, OWN), BF), pltpu.SemaphoreType.DMA((FRONT_SEMS,)),
    ]


def front(ins, gz_ref, scratch):
    own_from, lo_ref, hi_ref, first_lo, first_hi, pre_from, coarse_pre_from, coarse_w_from = ins
    coarse_gz, fine_store, coarse_store, pre, coarse_pre, coarse_w, spread, own, sems = scratch
    fine, coarse = pl.ds(0, D * NF), pl.ds(D * NF, 2 * NC)
    loads = [
        pltpu.make_async_copy(source, target, sems.at[at])
        for at, (source, target) in enumerate((
            (own_from.at[:, coarse], own.at[:, coarse]),
            (coarse_pre_from.at[:, pl.ds(0, 6 * NC)], coarse_pre),
            (coarse_w_from, coarse_w),
            (first_lo.at[:, pl.ds(EDGE, NF)], pre.at[:, pl.ds(0, NF)]),
            (pre_from, pre.at[:, pl.ds(NF, D * NF)]),
            (first_hi.at[:, pl.ds(EDGE, NF)], pre.at[:, pl.ds(5 * NF, NF)]),
            (own_from.at[:, fine], own.at[:, fine]),
        ))
    ]
    for load in loads:
        load.start()
    spread[...] = spread_matrix()
    for load in loads[:2]:
        load.wait()
    for j in range(6):
        source = (lo_ref, own, hi_ref)[j // 2]
        base = (NF, D * NF, NF)[j // 2] + (j % 2) * NC
        pooled = source[:, base : base + NC].astype(F32)
        mask = coarse_pre[:, j * NC : (j + 1) * NC].astype(F32) > 0
        gz = jnp.where(mask, pooled, 0.0)
        coarse_gz[:, j * NC : (j + 1) * NC] = gz.astype(BF)
        store_cross_shifts(coarse_store, gz, j * 3 * C, NC, HX)
    loads[2].wait()
    backs = []
    for j in range(4):
        taps = dot(coarse_w[...], coarse_store[j * 3 * C : (j + 3) * 3 * C, :])
        backs.append(inline_sum(taps, HX).astype(BF))
    spreads = dot(jnp.concatenate(backs, axis=0), spread[...])
    for load in loads[3:]:
        load.wait()
    for d in range(6):
        if d == 0:
            grad = lo_ref[:, :NF]
        elif d == 5:
            grad = hi_ref[:, :NF]
        else:
            grad = own[:, (d - 1) * NF : d * NF]
        j = (d + 1) // 2
        total = grad.astype(F32) + 0.125 * spreads[j * C : (j + 1) * C]
        gz = jnp.where(pre[:, d * NF : (d + 1) * NF].astype(F32) > 0, total, 0.0).astype(BF)
        gz_ref[:, d * NF : (d + 1) * NF] = gz
        store_cross_shifts(fine_store, gz.astype(F32), d * 3 * C, NF, XL)


def fine_slab(d, own, fine_w, fine_store):
    taps = dot(fine_w[...], fine_store[d * 3 * C : (d + 3) * 3 * C, :])
    grad = own[:, d * NF : (d + 1) * NF].astype(F32)
    return (grad + inline_sum(taps, XL)).astype(BF)


def turn_kernel(act_ref, *refs):
    ins, fine_w_from, outs = refs[: FRONT_INS - 1], refs[FRONT_INS - 1], refs[-18:]
    own_out, up_out, down_out, keep_gz, keep_coarse_gz, keep_grad = outs[:6]
    gz, fine_w, sems = outs[6:9]
    scratch = outs[9:]
    coarse_gz, fine_store, spread, own = scratch[0], scratch[1], scratch[6], scratch[7]

    @pl.when(act_ref[0] == 1)
    def _():
        weights = pltpu.make_async_copy(fine_w_from, fine_w, sems.at[0])
        weights.start()
        front(ins, gz, scratch)
        saves = [
            pltpu.make_async_copy(gz, keep_gz, sems.at[1]),
            pltpu.make_async_copy(coarse_gz, keep_coarse_gz, sems.at[2]),
        ]
        for save in saves:
            save.start()
        weights.wait()
        slabs = []
        for d in range(D):
            slabs.append(fine_slab(d, own, fine_w, fine_store))
            own_out[:, d * NF : (d + 1) * NF] = slabs[d]
        fine = pl.ds(0, D * NF)
        saves.append(pltpu.make_async_copy(own_out.at[:, fine], keep_grad, sems.at[3]))
        saves[-1].start()
        write_edges(slabs, spread, own_out.at[:, pl.ds(D * NF, 2 * NC)], up_out, down_out)
        for save in saves:
            save.wait()


def last_kernel(act_ref, *refs):
    ins = refs[: FRONT_INS - 1]
    keep_gz, keep_coarse_gz, saved_from, out_ref, gz, saved, coarse_saved, sems = refs[FRONT_INS - 1 : FRONT_INS + 7]
    scratch = refs[FRONT_INS + 7 :]
    coarse_gz, fine_store, coarse_store = scratch[:3]
    loads = [
        pltpu.make_async_copy(saved_from, saved, sems.at[0]),
        pltpu.make_async_copy(ins[6].at[:, pl.ds(6 * NC, 2 * NC)], coarse_saved, sems.at[1]),
    ]

    for load in loads:
        load.start()

    @pl.when(act_ref[0] == 1)
    def _():
        front(ins, gz, scratch)

    @pl.when(act_ref[0] == 0)
    def _():
        kept = [
            pltpu.make_async_copy(keep_gz, gz, sems.at[2]),
            pltpu.make_async_copy(keep_coarse_gz, coarse_gz, sems.at[3]),
        ]
        for copy in kept:
            copy.start()
        for copy in kept:
            copy.wait()
        for j in range(6):
            store_cross_shifts(
                coarse_store, coarse_gz[:, j * NC : (j + 1) * NC].astype(F32), j * 3 * C, NC, HX
            )
        for d in range(6):
            store_cross_shifts(fine_store, gz[:, d * NF : (d + 1) * NF].astype(F32), d * 3 * C, NF, XL)

    for load in loads:
        load.wait()
    fine_total = None
    for d in range(D):
        moved = inline_shifts(saved[:, d * NF : (d + 1) * NF], XL)
        term = dot_nt(moved, fine_store[d * 3 * C : (d + 3) * 3 * C, :])
        fine_total = term if fine_total is None else fine_total + term
    total = None
    for j in range(2):
        moved = inline_shifts(coarse_saved[:, j * NC : (j + 1) * NC], HX)
        term = dot_nt(moved, coarse_store[(j + 1) * 3 * C : (j + 4) * 3 * C, :])
        total = term if total is None else total + term
    out_ref[27 * C :, :] = jnp.zeros((C, 2 * C), BF)
    for inline_tap in range(3):
        for column in range(9):
            depth_tap, cross_tap = 2 - column // 3, column % 3
            tap = depth_tap * 9 + inline_tap * 3 + cross_tap
            rows, lanes = slice(inline_tap * C, (inline_tap + 1) * C), slice(column * C, (column + 1) * C)
            both = jnp.concatenate([fine_total[rows, lanes], total[rows, lanes]], axis=1)
            out_ref[tap * C : (tap + 1) * C, :] = both.astype(BF)


def grad_kernel(act_ref, gz, own, fine_w, kept, keep_grad, new, fine_store, sem):
    @pl.when(act_ref[0] == 1)
    def _():
        for d in range(6):
            store_cross_shifts(fine_store, gz[:, d * NF : (d + 1) * NF].astype(F32), d * 3 * C, NF, XL)
        for d in range(D):
            new[:, d * NF : (d + 1) * NF] = fine_slab(d, own, fine_w, fine_store)
        save = pltpu.make_async_copy(new, keep_grad, sem.at[0])
        save.start()
        save.wait()


VM = pl.BlockSpec(memory_space=pltpu.VMEM)
SM = pl.BlockSpec(memory_space=pltpu.SMEM)
HB = pl.BlockSpec(memory_space=pl.ANY)


def call(kernel, vmem, outs, ins, scratch, flops, args, keeps=(), aliases={}):
    moved = sum(a.size * a.dtype.itemsize for a in args)
    return pl.pallas_call(
        kernel,
        out_shape=[jax.ShapeDtypeStruct(shape, BF) for shape in tuple(outs) + tuple(keeps)],
        in_specs=ins,
        out_specs=[VM] * len(outs) + [HB] * len(keeps),
        scratch_shapes=scratch,
        input_output_aliases=aliases,
        compiler_params=pltpu.CompilerParams(vmem_limit_bytes=vmem),
        cost_estimate=pl.CostEstimate(flops=flops, bytes_accessed=moved, transcendentals=0),
    )(*args)


def pack_rows(mask, saved):
    vols = lax.axis_size("vol")
    pairs = mask.reshape(C, vols, 2 * HX)
    padded = jnp.pad(pairs, ((0, 0), (1, 1), (0, 0)))
    parts = [padded[:, k : k + vols] for k in range(3)] + [saved.reshape(C, vols, 2 * HX)]
    return jnp.concatenate(parts, axis=2)


def depth_slices(packed):
    vols = lax.axis_size("vol")
    moved = lax.all_to_all(packed, "vol", split_axis=1, concat_axis=1, tiled=True)
    return jnp.transpose(moved.reshape(C, vols, 8, HX), (0, 2, 1, 3)).reshape(C, 8 * NC)


def hop(array, pairs):
    return lax.ppermute(array, ("segment", "vol"), pairs)


def reduce_all(partial):
    vols = lax.axis_size("vol")
    part = partial.reshape(vols, partial.shape[0] // vols, partial.shape[1])
    part = lax.all_to_all(part, "vol", 0, 0)
    part = part.astype(F32).sum(axis=0).astype(BF)
    part = jnp.broadcast_to(part[None], (vols,) + part.shape)
    part = lax.all_to_all(part, "vol", 0, 0)
    return part.reshape(partial.shape)


def on_device(
    cotangent, labels, class_weight, inputs, fine_pre, pooled, coarse_pre, fine_filters, coarse_filters
):
    segments = lax.axis_size("segment")
    vols = lax.axis_size("vol")
    position = lax.axis_index("segment")
    pre = fine_pre[0].reshape(C, D * NF)
    head_edge = EDGE + NF
    at = lax.axis_index("vol")
    own, even, odd = call(
        functools.partial(seed_kernel, vols - 1), SEED_VMEM,
        [(C, OWN), (C, head_edge), (C, head_edge)], [SM, SM, VM, VM, VM],
        [pltpu.VMEM((NC, NF), BF)], 10**9,
        (class_weight, at.astype(jnp.int32).reshape(1), cotangent.reshape(C, D * NF), labels, pre),
    )
    odd = lax.ppermute(odd, "vol", [(v, (v + (1 if v % 2 else -1)) % vols) for v in range(vols)])
    even = lax.ppermute(even, "vol", [(v, v ^ 1) for v in range(vols)])
    first_lo = jnp.where(at % 2 == 0, odd, even)
    first_hi = jnp.where(at % 2 == 0, even, odd)
    coarse_both = depth_slices(pack_rows(coarse_pre[0], pooled[0]))
    coarse_both, saved = lax.optimization_barrier((coarse_both, inputs[0].reshape(C, D * NF)))
    fine_w = filter_matrix(fine_filters[0])
    coarse_w = filter_matrix(coarse_filters[0])
    lo, hi = first_lo, first_hi
    keeps = ()
    for turn in range(segments - 1):
        s = segments - 1 - turn
        act = (position == s).astype(jnp.int32).reshape(1)
        own, up, down, *keeps = call(
            turn_kernel, TURN_VMEM,
            [(C, OWN), (C, EDGE), (C, EDGE)],
            [SM, HB, VM, VM] + [HB] * (6 + len(keeps)),
            [
                pltpu.VMEM((C, 6 * NF), BF), pltpu.VMEM((3 * C, 9 * C), BF), pltpu.SemaphoreType.DMA((4,)),
                *front_scratch(),
            ],
            4 * 10**9,
            (act, own, lo, hi, first_lo, first_hi, pre, coarse_both, coarse_w, fine_w, *keeps),
            ((C, 6 * NF), (C, 6 * NC), (C, D * NF)),
            {10 + k: 3 + k for k in range(len(keeps))},
        )
        base, to = s * vols, (s - 1) * vols
        lo = hop(up, [(base + v, to + v + 1) for v in range(vols - 1)])
        hi = hop(down, [(base + v + 1, to + v) for v in range(vols - 1)])
        own = hop(own, [(base + v, to + v) for v in range(vols)])
    act = (position == 0).astype(jnp.int32).reshape(1)
    keep_gz, keep_coarse_gz, keep_grad = keeps
    partial, gz = call(
        last_kernel, LAST_VMEM,
        [(28 * C, 2 * C), (C, 6 * NF)],
        [SM, HB, VM, VM] + [HB] * 8,
        [
            pltpu.VMEM((C, D * NF), BF), pltpu.VMEM((C, 2 * NC), BF), pltpu.SemaphoreType.DMA((4,)),
            *front_scratch(),
        ],
        4 * 10**9,
        (
            act, own, lo, hi, first_lo, first_hi, pre, coarse_both, coarse_w,
            keep_gz, keep_coarse_gz, saved,
        ),
    )
    (grad,) = call(
        grad_kernel, GRAD_VMEM, [], [SM, VM, VM, VM, HB],
        [pltpu.VMEM((C, D * NF), BF), pltpu.VMEM((18 * C, NF), BF), pltpu.SemaphoreType.DMA((1,))],
        2 * 10**9, (act, gz, own, fine_w, keep_grad), ((C, D * NF),), {4: 0},
    )
    total = reduce_all(partial)
    cells = D * vols * NF
    total = total[: 27 * C].reshape(27, C, 2 * C).astype(F32)
    fine_total = total[:, :, :C] * (1.0 / math.sqrt(cells))
    coarse_total = total[:, :, C:] * (1.0 / math.sqrt(cells // 8))
    return grad.reshape(1, C, D, NF), fine_total[None], coarse_total[None]


def solution(mesh):
    return jax.shard_map(
        on_device,
        mesh=mesh,
        in_specs=(
            P(None, "vol", None),
            P("vol", None),
            P(),
            P("segment", None, "vol", None),
            P("segment", None, "vol", None),
            P("segment", None, "vol", None),
            P("segment", None, "vol", None),
            P("segment", None, None, None),
            P("segment", None, None, None),
        ),
        out_specs=(
            P("segment", None, "vol", None),
            P("segment", None, None, None),
            P("segment", None, None, None),
        ),
        check_vma=False,
    )
```

```python
import functools
import math

import jax
import jax.numpy as jnp
from jax import lax
from jax.experimental import pallas as pl
from jax.experimental.pallas import tpu as pltpu
from jax.sharding import PartitionSpec as P

XL = 16
HX = XL // 2
C = 64
D = 4
NF = 1024
NC = 256
EDGE = NF + 2 * NC
OWN = D * NF + 2 * NC
BF = jnp.bfloat16
F32 = jnp.float32
SEED_VMEM = 58000 * 1024
TURN_VMEM = 52600 * 1024
LAST_VMEM = 52600 * 1024
GRAD_VMEM = 52600 * 1024


def spread_matrix():
    coarse = lax.broadcasted_iota(jnp.int32, (NC, NF), 0)
    fine = lax.broadcasted_iota(jnp.int32, (NC, NF), 1)
    owner = (fine // (2 * XL)) * HX + (fine % XL) // 2
    return jnp.where(coarse == owner, 1.0, 0.0).astype(BF)


def filter_matrix(weights):
    grid = weights.reshape(3, 3, 3, C, C)[::-1]
    return jnp.transpose(grid, (1, 3, 0, 2, 4)).reshape(3 * C, 9 * C)


def dot(a, b):
    return jnp.dot(a, b, preferred_element_type=F32)


def dot_nt(a, b):
    return lax.dot_general(a, b, (((1,), (1,)), ((), ())), preferred_element_type=F32)


def store_cross_shifts(store, slab, row, width, columns):
    column = lax.broadcasted_iota(jnp.int32, (C, 128), 1) % columns
    for at in range(0, width, 128):
        part = slab[:, at : at + 128]
        back = jnp.where(column < columns - 1, pltpu.roll(part, 127, 1), 0.0)
        ahead = jnp.where(column > 0, pltpu.roll(part, 1, 1), 0.0)
        store[row : row + C, at : at + 128] = back.astype(BF)
        store[row + C : row + 2 * C, at : at + 128] = part.astype(BF)
        store[row + 2 * C : row + 3 * C, at : at + 128] = ahead.astype(BF)


def inline_sum(taps, columns):
    width = taps.shape[1]
    lane = lax.broadcasted_iota(jnp.int32, (C, width), 1)
    first = jnp.where(lane < width - columns, pltpu.roll(taps[:C], width - columns, 1), 0.0)
    last = jnp.where(lane >= columns, pltpu.roll(taps[2 * C :], columns, 1), 0.0)
    return taps[C : 2 * C] + first + last


def inline_shifts(saved, columns):
    wide = saved.astype(F32)
    width = wide.shape[1]
    lane = lax.broadcasted_iota(jnp.int32, (C, width), 1)
    first = jnp.where(lane >= columns, pltpu.roll(wide, columns, 1), 0.0)
    last = jnp.where(lane < width - columns, pltpu.roll(wide, width - columns, 1), 0.0)
    return jnp.concatenate([first.astype(BF), saved, last.astype(BF)], axis=0)


def write_edges(slabs, spread, pooled_ref, up_ref, down_ref):
    down_ref[:, :NF] = slabs[0]
    up_ref[:, :NF] = slabs[D - 1]
    sums = dot_nt(jnp.concatenate(slabs, axis=0), spread[...])
    for j in range(2):
        at = 2 * j * C
        pooled = (sums[at : at + C] + sums[at + C : at + 2 * C]).astype(BF)
        pooled_ref[:, j * NC : (j + 1) * NC] = pooled
        down_ref[:, NF + j * NC : NF + (j + 1) * NC] = pooled
        up_ref[:, NF + j * NC : NF + (j + 1) * NC] = pooled


def seed_kernel(weight_ref, cot_ref, label_ref, pre_ref, own_ref, up_ref, down_ref, spread_ref):
    spread_ref[...] = spread_matrix()
    slabs = []
    for d in range(D):
        label = label_ref[d : d + 1, :]
        weight = jnp.zeros(label.shape, F32)
        for k in range(3):
            weight = weight + jnp.where(label == k, weight_ref[k], 0.0)
        slabs.append((cot_ref[:, d * NF : (d + 1) * NF].astype(F32) * weight).astype(BF))
        own_ref[:, d * NF : (d + 1) * NF] = slabs[d]
    write_edges(slabs, spread_ref, own_ref.at[:, pl.ds(D * NF, 2 * NC)], up_ref, down_ref)
    down_ref[:, EDGE:] = pre_ref[:, :NF]
    up_ref[:, EDGE:] = pre_ref[:, (D - 1) * NF :]


FRONT_INS = 10
FRONT_SEMS = 8


def front_scratch():
    return [
        pltpu.VMEM((C, 6 * NC), BF), pltpu.VMEM((18 * C, NF), BF), pltpu.VMEM((18 * C, NC), BF),
        pltpu.VMEM((C, 6 * NF), BF), pltpu.VMEM((C, 6 * NC), BF), pltpu.VMEM((3 * C, 9 * C), BF),
        pltpu.VMEM((NC, NF), BF), pltpu.VMEM((C, OWN), BF), pltpu.SemaphoreType.DMA((FRONT_SEMS,)),
    ]


def front(ins, gz_ref, scratch):
    own_from, lo_ref, hi_ref, first_lo, first_hi, pre_from, coarse_pre_from, coarse_w_from, spread_from = ins
    coarse_gz, fine_store, coarse_store, pre, coarse_pre, coarse_w, spread, own, sems = scratch
    fine, coarse = pl.ds(0, D * NF), pl.ds(D * NF, 2 * NC)
    loads = [
        pltpu.make_async_copy(source, target, sems.at[at])
        for at, (source, target) in enumerate((
            (own_from.at[:, coarse], own.at[:, coarse]),
            (coarse_pre_from.at[:, pl.ds(0, 6 * NC)], coarse_pre),
            (coarse_w_from, coarse_w),
            (spread_from, spread),
            (first_lo.at[:, pl.ds(EDGE, NF)], pre.at[:, pl.ds(0, NF)]),
            (pre_from, pre.at[:, pl.ds(NF, D * NF)]),
            (first_hi.at[:, pl.ds(EDGE, NF)], pre.at[:, pl.ds(5 * NF, NF)]),
            (own_from.at[:, fine], own.at[:, fine]),
        ))
    ]
    for load in loads:
        load.start()
    for load in loads[:2]:
        load.wait()
    for j in range(6):
        source = (lo_ref, own, hi_ref)[j // 2]
        base = (NF, D * NF, NF)[j // 2] + (j % 2) * NC
        pooled = source[:, base : base + NC].astype(F32)
        mask = coarse_pre[:, j * NC : (j + 1) * NC].astype(F32) > 0
        gz = jnp.where(mask, pooled, 0.0)
        coarse_gz[:, j * NC : (j + 1) * NC] = gz.astype(BF)
        store_cross_shifts(coarse_store, gz, j * 3 * C, NC, HX)
    loads[2].wait()
    backs = []
    for j in range(4):
        taps = dot(coarse_w[...], coarse_store[j * 3 * C : (j + 3) * 3 * C, :])
        backs.append(inline_sum(taps, HX).astype(BF))
    loads[3].wait()
    spreads = dot(jnp.concatenate(backs, axis=0), spread[...])
    for load in loads[4:]:
        load.wait()
    for d in range(6):
        if d == 0:
            grad = lo_ref[:, :NF]
        elif d == 5:
            grad = hi_ref[:, :NF]
        else:
            grad = own[:, (d - 1) * NF : d * NF]
        j = (d + 1) // 2
        total = grad.astype(F32) + 0.125 * spreads[j * C : (j + 1) * C]
        gz = jnp.where(pre[:, d * NF : (d + 1) * NF].astype(F32) > 0, total, 0.0).astype(BF)
        gz_ref[:, d * NF : (d + 1) * NF] = gz
        store_cross_shifts(fine_store, gz.astype(F32), d * 3 * C, NF, XL)


def fine_slab(d, own, fine_w, fine_store):
    taps = dot(fine_w[...], fine_store[d * 3 * C : (d + 3) * 3 * C, :])
    grad = own[:, d * NF : (d + 1) * NF].astype(F32)
    return (grad + inline_sum(taps, XL)).astype(BF)


def turn_kernel(act_ref, *refs):
    ins, fine_w_from, outs = refs[: FRONT_INS - 1], refs[FRONT_INS - 1], refs[-19:]
    up_out, down_out, own_out, keep_gz, keep_coarse_gz, keep_grad = outs[:6]
    gz, fine_w, new, sems = outs[6:10]
    scratch = outs[10:]
    coarse_gz, fine_store, spread, own = scratch[0], scratch[1], scratch[6], scratch[7]

    @pl.when(act_ref[0] == 1)
    def _():
        weights = pltpu.make_async_copy(fine_w_from, fine_w, sems.at[0])
        weights.start()
        front(ins, gz, scratch)
        saves = [
            pltpu.make_async_copy(gz, keep_gz, sems.at[1]),
            pltpu.make_async_copy(coarse_gz, keep_coarse_gz, sems.at[2]),
        ]
        for save in saves:
            save.start()
        weights.wait()
        slabs = []
        for d in range(D):
            slabs.append(fine_slab(d, own, fine_w, fine_store))
            lanes = pl.ds(d * NF, NF)
            new[:, d * NF : (d + 1) * NF] = slabs[d]
            for at, target in ((3 + d, own_out), (3 + D + d, keep_grad)):
                saves.append(pltpu.make_async_copy(new.at[:, lanes], target.at[:, lanes], sems.at[at]))
                saves[-1].start()
        lanes = pl.ds(D * NF, 2 * NC)
        write_edges(slabs, spread, new.at[:, lanes], up_out, down_out)
        saves.append(pltpu.make_async_copy(new.at[:, lanes], own_out.at[:, lanes], sems.at[3 + 2 * D]))
        saves[-1].start()
        for save in saves:
            save.wait()


def last_kernel(act_ref, *refs):
    ins = refs[: FRONT_INS - 1]
    keep_gz, keep_coarse_gz, saved_from, out_ref, gz, saved, coarse_saved, sems = refs[FRONT_INS - 1 : FRONT_INS + 7]
    scratch = refs[FRONT_INS + 7 :]
    coarse_gz, fine_store, coarse_store = scratch[:3]
    loads = [
        pltpu.make_async_copy(saved_from, saved, sems.at[0]),
        pltpu.make_async_copy(ins[6].at[:, pl.ds(6 * NC, 2 * NC)], coarse_saved, sems.at[1]),
    ]

    for load in loads:
        load.start()

    @pl.when(act_ref[0] == 1)
    def _():
        front(ins, gz, scratch)

    @pl.when(act_ref[0] == 0)
    def _():
        kept = [
            pltpu.make_async_copy(keep_gz, gz, sems.at[2]),
            pltpu.make_async_copy(keep_coarse_gz, coarse_gz, sems.at[3]),
        ]
        for copy in kept:
            copy.start()
        for copy in kept:
            copy.wait()
        for j in range(6):
            store_cross_shifts(
                coarse_store, coarse_gz[:, j * NC : (j + 1) * NC].astype(F32), j * 3 * C, NC, HX
            )
        for d in range(6):
            store_cross_shifts(fine_store, gz[:, d * NF : (d + 1) * NF].astype(F32), d * 3 * C, NF, XL)

    for load in loads:
        load.wait()
    fine_total = None
    for d in range(D):
        moved = inline_shifts(saved[:, d * NF : (d + 1) * NF], XL)
        term = dot_nt(moved, fine_store[d * 3 * C : (d + 3) * 3 * C, :])
        fine_total = term if fine_total is None else fine_total + term
    total = None
    for j in range(2):
        moved = inline_shifts(coarse_saved[:, j * NC : (j + 1) * NC], HX)
        term = dot_nt(moved, coarse_store[(j + 1) * 3 * C : (j + 4) * 3 * C, :])
        total = term if total is None else total + term
    for inline_tap in range(3):
        for column in range(9):
            depth_tap, cross_tap = 2 - column // 3, column % 3
            tap = depth_tap * 9 + inline_tap * 3 + cross_tap
            rows, lanes = slice(inline_tap * C, (inline_tap + 1) * C), slice(column * C, (column + 1) * C)
            both = jnp.concatenate([fine_total[rows, lanes], total[rows, lanes]], axis=1)
            out_ref[tap * C : (tap + 1) * C, :] = both.astype(BF)


def grad_kernel(act_ref, gz, own, fine_w, kept, keep_grad, new, fine_store, sem):
    @pl.when(act_ref[0] == 1)
    def _():
        for d in range(6):
            store_cross_shifts(fine_store, gz[:, d * NF : (d + 1) * NF].astype(F32), d * 3 * C, NF, XL)
        for d in range(D):
            new[:, d * NF : (d + 1) * NF] = fine_slab(d, own, fine_w, fine_store)
        save = pltpu.make_async_copy(new, keep_grad, sem.at[0])
        save.start()
        save.wait()


VM = pl.BlockSpec(memory_space=pltpu.VMEM)
SM = pl.BlockSpec(memory_space=pltpu.SMEM)
HB = pl.BlockSpec(memory_space=pl.ANY)


def call(kernel, vmem, outs, ins, scratch, flops, args, keeps=(), aliases={}):
    moved = sum(a.size * a.dtype.itemsize for a in args)
    return pl.pallas_call(
        kernel,
        out_shape=[jax.ShapeDtypeStruct(shape, BF) for shape in tuple(outs) + tuple(keeps)],
        in_specs=ins,
        out_specs=[VM] * len(outs) + [HB] * len(keeps),
        scratch_shapes=scratch,
        input_output_aliases=aliases,
        compiler_params=pltpu.CompilerParams(vmem_limit_bytes=vmem),
        cost_estimate=pl.CostEstimate(flops=flops, bytes_accessed=moved, transcendentals=0),
    )(*args)


def pack_rows(mask, saved):
    vols = lax.axis_size("vol")
    pairs = mask.reshape(C, vols, 2 * HX)
    padded = jnp.pad(pairs, ((0, 0), (1, 1), (0, 0)))
    parts = [padded[:, k : k + vols] for k in range(3)] + [saved.reshape(C, vols, 2 * HX)]
    return jnp.concatenate(parts, axis=2)


def depth_slices(packed):
    vols = lax.axis_size("vol")
    moved = lax.all_to_all(packed, "vol", split_axis=1, concat_axis=1, tiled=True)
    return jnp.transpose(moved.reshape(C, vols, 8, HX), (0, 2, 1, 3)).reshape(C, 8 * NC)


def hop(array, pairs):
    return lax.ppermute(array, ("segment", "vol"), pairs)


def reduce_all(partial):
    vols = lax.axis_size("vol")
    part = partial.reshape(vols, partial.shape[0] // vols, partial.shape[1])
    part = lax.all_to_all(part, "vol", 0, 0)
    part = part.astype(F32).sum(axis=0).astype(BF)
    part = jnp.broadcast_to(part[None], (vols,) + part.shape)
    part = lax.all_to_all(part, "vol", 0, 0)
    return part.reshape(partial.shape)


def on_device(
    cotangent, labels, class_weight, inputs, fine_pre, pooled, coarse_pre, fine_filters, coarse_filters
):
    segments = lax.axis_size("segment")
    vols = lax.axis_size("vol")
    position = lax.axis_index("segment")
    pre = fine_pre[0].reshape(C, D * NF)
    head_edge = EDGE + NF
    own, up, down, spread = call(
        seed_kernel, SEED_VMEM, [(C, OWN), (C, head_edge), (C, head_edge), (NC, NF)], [SM, VM, VM, VM], [], 10**9,
        (class_weight, cotangent.reshape(C, D * NF), labels, pre),
    )
    first_lo = lax.ppermute(up, "vol", [(v, v + 1) for v in range(vols - 1)])
    first_hi = lax.ppermute(down, "vol", [(v + 1, v) for v in range(vols - 1)])
    coarse_both = depth_slices(pack_rows(coarse_pre[0], pooled[0]))
    fine_w = filter_matrix(fine_filters[0])
    coarse_w = filter_matrix(coarse_filters[0])
    lo, hi = first_lo, first_hi
    keeps = ()
    for turn in range(segments - 1):
        s = segments - 1 - turn
        act = (position == s).astype(jnp.int32).reshape(1)
        up, down, own, *keeps = call(
            turn_kernel, TURN_VMEM,
            [(C, EDGE), (C, EDGE)],
            [SM, HB, VM, VM] + [HB] * (7 + len(keeps)),
            [
                pltpu.VMEM((C, 6 * NF), BF), pltpu.VMEM((3 * C, 9 * C), BF), pltpu.VMEM((C, OWN), BF),
                pltpu.SemaphoreType.DMA((4 + 2 * D,)), *front_scratch(),
            ],
            4 * 10**9,
            (act, own, lo, hi, first_lo, first_hi, pre, coarse_both, coarse_w, spread, fine_w, *keeps),
            ((C, OWN), (C, 6 * NF), (C, 6 * NC), (C, D * NF)),
            {11 + k: 3 + k for k in range(len(keeps))},
        )
        base, to = s * vols, (s - 1) * vols
        lo = hop(up, [(base + v, to + v + 1) for v in range(vols - 1)])
        hi = hop(down, [(base + v + 1, to + v) for v in range(vols - 1)])
        own = hop(own, [(base + v, to + v) for v in range(vols)])
    act = (position == 0).astype(jnp.int32).reshape(1)
    keep_gz, keep_coarse_gz, keep_grad = keeps
    partial, gz = call(
        last_kernel, LAST_VMEM,
        [(27 * C, 2 * C), (C, 6 * NF)],
        [SM, HB, VM, VM] + [HB] * 9,
        [
            pltpu.VMEM((C, D * NF), BF), pltpu.VMEM((C, 2 * NC), BF), pltpu.SemaphoreType.DMA((4,)),
            *front_scratch(),
        ],
        4 * 10**9,
        (
            act, own, lo, hi, first_lo, first_hi, pre, coarse_both, coarse_w, spread,
            keep_gz, keep_coarse_gz, inputs[0].reshape(C, D * NF),
        ),
    )
    (grad,) = call(
        grad_kernel, GRAD_VMEM, [], [SM, VM, VM, VM, HB],
        [pltpu.VMEM((C, D * NF), BF), pltpu.VMEM((18 * C, NF), BF), pltpu.SemaphoreType.DMA((1,))],
        2 * 10**9, (act, gz, own, fine_w, keep_grad), ((C, D * NF),), {4: 0},
    )
    total = reduce_all(partial)
    cells = D * vols * NF
    total = total.reshape(27, C, 2 * C).astype(F32)
    fine_total = total[:, :, :C] * (1.0 / math.sqrt(cells))
    coarse_total = total[:, :, C:] * (1.0 / math.sqrt(cells // 8))
    return grad.reshape(1, C, D, NF), fine_total[None], coarse_total[None]


def solution(mesh):
    return jax.shard_map(
        on_device,
        mesh=mesh,
        in_specs=(
            P(None, "vol", None),
            P("vol", None),
            P(),
            P("segment", None, "vol", None),
            P("segment", None, "vol", None),
            P("segment", None, "vol", None),
            P("segment", None, "vol", None),
            P("segment", None, None, None),
            P("segment", None, None, None),
        ),
        out_specs=(
            P("segment", None, "vol", None),
            P("segment", None, None, None),
            P("segment", None, None, None),
        ),
        check_vma=False,
    )
```

```python
import functools
import math

import jax
import jax.numpy as jnp
from jax import lax
from jax.experimental import pallas as pl
from jax.experimental.pallas import tpu as pltpu
from jax.sharding import PartitionSpec as P

XL = 16
HX = XL // 2
C = 64
D = 4
NF = 1024
NC = 256
EDGE = NF + 2 * NC
OWN = D * NF + 2 * NC
BF = jnp.bfloat16
F32 = jnp.float32
SEED_VMEM = 58000 * 1024
TURN_VMEM = 51500 * 1024
LAST_VMEM = 51500 * 1024
GRAD_VMEM = 51500 * 1024


def spread_matrix():
    coarse = lax.broadcasted_iota(jnp.int32, (NC, NF), 0)
    fine = lax.broadcasted_iota(jnp.int32, (NC, NF), 1)
    owner = (fine // (2 * XL)) * HX + (fine % XL) // 2
    return jnp.where(coarse == owner, 1.0, 0.0).astype(BF)


def filter_matrix(weights):
    grid = weights.reshape(3, 3, 3, C, C)[::-1]
    return jnp.transpose(grid, (1, 3, 0, 2, 4)).reshape(3 * C, 9 * C)


def dot(a, b):
    return jnp.dot(a, b, preferred_element_type=F32)


def dot_nt(a, b):
    return lax.dot_general(a, b, (((1,), (1,)), ((), ())), preferred_element_type=F32)


def store_cross_shifts(store, slab, row, width, columns):
    column = lax.broadcasted_iota(jnp.int32, (C, 128), 1) % columns
    for at in range(0, width, 128):
        part = slab[:, at : at + 128]
        back = jnp.where(column < columns - 1, pltpu.roll(part, 127, 1), 0.0)
        ahead = jnp.where(column > 0, pltpu.roll(part, 1, 1), 0.0)
        store[row : row + C, at : at + 128] = back.astype(BF)
        store[row + C : row + 2 * C, at : at + 128] = part.astype(BF)
        store[row + 2 * C : row + 3 * C, at : at + 128] = ahead.astype(BF)


def inline_sum(taps, columns):
    width = taps.shape[1]
    lane = lax.broadcasted_iota(jnp.int32, (C, width), 1)
    first = jnp.where(lane < width - columns, pltpu.roll(taps[:C], width - columns, 1), 0.0)
    last = jnp.where(lane >= columns, pltpu.roll(taps[2 * C :], columns, 1), 0.0)
    return taps[C : 2 * C] + first + last


def inline_shifts(saved, columns):
    wide = saved.astype(F32)
    width = wide.shape[1]
    lane = lax.broadcasted_iota(jnp.int32, (C, width), 1)
    first = jnp.where(lane >= columns, pltpu.roll(wide, columns, 1), 0.0)
    last = jnp.where(lane < width - columns, pltpu.roll(wide, width - columns, 1), 0.0)
    return jnp.concatenate([first.astype(BF), saved, last.astype(BF)], axis=0)


def write_edges(slabs, spread, pooled_ref, up_ref, down_ref):
    down_ref[:, :NF] = slabs[0]
    up_ref[:, :NF] = slabs[D - 1]
    sums = dot_nt(jnp.concatenate(slabs, axis=0), spread[...])
    for j in range(2):
        at = 2 * j * C
        pooled = (sums[at : at + C] + sums[at + C : at + 2 * C]).astype(BF)
        pooled_ref[:, j * NC : (j + 1) * NC] = pooled
        down_ref[:, NF + j * NC : NF + (j + 1) * NC] = pooled
        up_ref[:, NF + j * NC : NF + (j + 1) * NC] = pooled


def seed_kernel(
    end, weight_ref, at_ref, cot_ref, label_ref, pre_ref, own_ref, even_ref, odd_ref, spread_ref
):
    spread_ref[...] = spread_matrix()
    slabs = []
    for d in range(D):
        label = label_ref[d : d + 1, :]
        weight = jnp.zeros(label.shape, F32)
        for k in range(3):
            weight = weight + jnp.where(label == k, weight_ref[k], 0.0)
        slabs.append((cot_ref[:, d * NF : (d + 1) * NF].astype(F32) * weight).astype(BF))
        own_ref[:, d * NF : (d + 1) * NF] = slabs[d]
    at = at_ref[0]
    pooled_ref = own_ref.at[:, pl.ds(D * NF, 2 * NC)]
    first, last = pre_ref[:, :NF], pre_ref[:, (D - 1) * NF :]

    @pl.when(at % 2 == 0)
    def _():
        write_edges(slabs, spread_ref, pooled_ref, even_ref, odd_ref)
        even_ref[:, EDGE:] = last
        odd_ref[:, EDGE:] = jnp.where(at == 0, 0.0, first.astype(F32)).astype(BF)

    @pl.when(at % 2 == 1)
    def _():
        write_edges(slabs, spread_ref, pooled_ref, odd_ref, even_ref)
        even_ref[:, EDGE:] = first
        odd_ref[:, EDGE:] = jnp.where(at == end, 0.0, last.astype(F32)).astype(BF)


FRONT_INS = 10
FRONT_SEMS = 8


def front_scratch():
    return [
        pltpu.VMEM((C, 6 * NC), BF), pltpu.VMEM((18 * C, NF), BF), pltpu.VMEM((18 * C, NC), BF),
        pltpu.VMEM((C, 6 * NF), BF), pltpu.VMEM((C, 6 * NC), BF), pltpu.VMEM((3 * C, 9 * C), BF),
        pltpu.VMEM((NC, NF), BF), pltpu.VMEM((C, OWN), BF), pltpu.SemaphoreType.DMA((FRONT_SEMS,)),
    ]


def front(ins, gz_ref, scratch):
    own_from, lo_ref, hi_ref, first_lo, first_hi, pre_from, coarse_pre_from, coarse_w_from, spread_from = ins
    coarse_gz, fine_store, coarse_store, pre, coarse_pre, coarse_w, spread, own, sems = scratch
    fine, coarse = pl.ds(0, D * NF), pl.ds(D * NF, 2 * NC)
    loads = [
        pltpu.make_async_copy(source, target, sems.at[at])
        for at, (source, target) in enumerate((
            (own_from.at[:, coarse], own.at[:, coarse]),
            (coarse_pre_from.at[:, pl.ds(0, 6 * NC)], coarse_pre),
            (coarse_w_from, coarse_w),
            (spread_from, spread),
            (first_lo.at[:, pl.ds(EDGE, NF)], pre.at[:, pl.ds(0, NF)]),
            (pre_from, pre.at[:, pl.ds(NF, D * NF)]),
            (first_hi.at[:, pl.ds(EDGE, NF)], pre.at[:, pl.ds(5 * NF, NF)]),
            (own_from.at[:, fine], own.at[:, fine]),
        ))
    ]
    for load in loads:
        load.start()
    for load in loads[:2]:
        load.wait()
    for j in range(6):
        source = (lo_ref, own, hi_ref)[j // 2]
        base = (NF, D * NF, NF)[j // 2] + (j % 2) * NC
        pooled = source[:, base : base + NC].astype(F32)
        mask = coarse_pre[:, j * NC : (j + 1) * NC].astype(F32) > 0
        gz = jnp.where(mask, pooled, 0.0)
        coarse_gz[:, j * NC : (j + 1) * NC] = gz.astype(BF)
        store_cross_shifts(coarse_store, gz, j * 3 * C, NC, HX)
    loads[2].wait()
    backs = []
    for j in range(4):
        taps = dot(coarse_w[...], coarse_store[j * 3 * C : (j + 3) * 3 * C, :])
        backs.append(inline_sum(taps, HX).astype(BF))
    loads[3].wait()
    spreads = dot(jnp.concatenate(backs, axis=0), spread[...])
    for load in loads[4:]:
        load.wait()
    for d in range(6):
        if d == 0:
            grad = lo_ref[:, :NF]
        elif d == 5:
            grad = hi_ref[:, :NF]
        else:
            grad = own[:, (d - 1) * NF : d * NF]
        j = (d + 1) // 2
        total = grad.astype(F32) + 0.125 * spreads[j * C : (j + 1) * C]
        gz = jnp.where(pre[:, d * NF : (d + 1) * NF].astype(F32) > 0, total, 0.0).astype(BF)
        gz_ref[:, d * NF : (d + 1) * NF] = gz
        store_cross_shifts(fine_store, gz.astype(F32), d * 3 * C, NF, XL)


def fine_slab(d, own, fine_w, fine_store):
    taps = dot(fine_w[...], fine_store[d * 3 * C : (d + 3) * 3 * C, :])
    grad = own[:, d * NF : (d + 1) * NF].astype(F32)
    return (grad + inline_sum(taps, XL)).astype(BF)


def turn_kernel(act_ref, *refs):
    ins, fine_w_from, outs = refs[: FRONT_INS - 1], refs[FRONT_INS - 1], refs[-19:]
    up_out, down_out, own_out, keep_gz, keep_coarse_gz, keep_grad = outs[:6]
    gz, fine_w, new, sems = outs[6:10]
    scratch = outs[10:]
    coarse_gz, fine_store, spread, own = scratch[0], scratch[1], scratch[6], scratch[7]

    @pl.when(act_ref[0] == 1)
    def _():
        weights = pltpu.make_async_copy(fine_w_from, fine_w, sems.at[0])
        weights.start()
        front(ins, gz, scratch)
        saves = [
            pltpu.make_async_copy(gz, keep_gz, sems.at[1]),
            pltpu.make_async_copy(coarse_gz, keep_coarse_gz, sems.at[2]),
        ]
        for save in saves:
            save.start()
        weights.wait()
        slabs = []
        for d in range(D):
            slabs.append(fine_slab(d, own, fine_w, fine_store))
            lanes = pl.ds(d * NF, NF)
            new[:, d * NF : (d + 1) * NF] = slabs[d]
            for at, target in ((3 + d, own_out), (3 + D + d, keep_grad)):
                saves.append(pltpu.make_async_copy(new.at[:, lanes], target.at[:, lanes], sems.at[at]))
                saves[-1].start()
        lanes = pl.ds(D * NF, 2 * NC)
        write_edges(slabs, spread, new.at[:, lanes], up_out, down_out)
        saves.append(pltpu.make_async_copy(new.at[:, lanes], own_out.at[:, lanes], sems.at[3 + 2 * D]))
        saves[-1].start()
        for save in saves:
            save.wait()


def last_kernel(act_ref, *refs):
    ins = refs[: FRONT_INS - 1]
    keep_gz, keep_coarse_gz, saved_from, out_ref, gz, saved, coarse_saved, sems = refs[FRONT_INS - 1 : FRONT_INS + 7]
    scratch = refs[FRONT_INS + 7 :]
    coarse_gz, fine_store, coarse_store = scratch[:3]
    loads = [
        pltpu.make_async_copy(saved_from, saved, sems.at[0]),
        pltpu.make_async_copy(ins[6].at[:, pl.ds(6 * NC, 2 * NC)], coarse_saved, sems.at[1]),
    ]

    for load in loads:
        load.start()

    @pl.when(act_ref[0] == 1)
    def _():
        front(ins, gz, scratch)

    @pl.when(act_ref[0] == 0)
    def _():
        kept = [
            pltpu.make_async_copy(keep_gz, gz, sems.at[2]),
            pltpu.make_async_copy(keep_coarse_gz, coarse_gz, sems.at[3]),
        ]
        for copy in kept:
            copy.start()
        for copy in kept:
            copy.wait()
        for j in range(6):
            store_cross_shifts(
                coarse_store, coarse_gz[:, j * NC : (j + 1) * NC].astype(F32), j * 3 * C, NC, HX
            )
        for d in range(6):
            store_cross_shifts(fine_store, gz[:, d * NF : (d + 1) * NF].astype(F32), d * 3 * C, NF, XL)

    for load in loads:
        load.wait()
    fine_total = None
    for d in range(D):
        moved = inline_shifts(saved[:, d * NF : (d + 1) * NF], XL)
        term = dot_nt(moved, fine_store[d * 3 * C : (d + 3) * 3 * C, :])
        fine_total = term if fine_total is None else fine_total + term
    total = None
    for j in range(2):
        moved = inline_shifts(coarse_saved[:, j * NC : (j + 1) * NC], HX)
        term = dot_nt(moved, coarse_store[(j + 1) * 3 * C : (j + 4) * 3 * C, :])
        total = term if total is None else total + term
    for inline_tap in range(3):
        for column in range(9):
            depth_tap, cross_tap = 2 - column // 3, column % 3
            tap = depth_tap * 9 + inline_tap * 3 + cross_tap
            rows, lanes = slice(inline_tap * C, (inline_tap + 1) * C), slice(column * C, (column + 1) * C)
            both = jnp.concatenate([fine_total[rows, lanes], total[rows, lanes]], axis=1)
            out_ref[tap * C : (tap + 1) * C, :] = both.astype(BF)


def grad_kernel(act_ref, gz, own, fine_w, kept, keep_grad, new, fine_store, sem):
    @pl.when(act_ref[0] == 1)
    def _():
        for d in range(6):
            store_cross_shifts(fine_store, gz[:, d * NF : (d + 1) * NF].astype(F32), d * 3 * C, NF, XL)
        for d in range(D):
            new[:, d * NF : (d + 1) * NF] = fine_slab(d, own, fine_w, fine_store)
        save = pltpu.make_async_copy(new, keep_grad, sem.at[0])
        save.start()
        save.wait()


VM = pl.BlockSpec(memory_space=pltpu.VMEM)
SM = pl.BlockSpec(memory_space=pltpu.SMEM)
HB = pl.BlockSpec(memory_space=pl.ANY)


def call(kernel, vmem, outs, ins, scratch, flops, args, keeps=(), aliases={}):
    moved = sum(a.size * a.dtype.itemsize for a in args)
    return pl.pallas_call(
        kernel,
        out_shape=[jax.ShapeDtypeStruct(shape, BF) for shape in tuple(outs) + tuple(keeps)],
        in_specs=ins,
        out_specs=[VM] * len(outs) + [HB] * len(keeps),
        scratch_shapes=scratch,
        input_output_aliases=aliases,
        compiler_params=pltpu.CompilerParams(vmem_limit_bytes=vmem),
        cost_estimate=pl.CostEstimate(flops=flops, bytes_accessed=moved, transcendentals=0),
    )(*args)


def pack_rows(mask, saved):
    vols = lax.axis_size("vol")
    pairs = mask.reshape(C, vols, 2 * HX)
    padded = jnp.pad(pairs, ((0, 0), (1, 1), (0, 0)))
    parts = [padded[:, k : k + vols] for k in range(3)] + [saved.reshape(C, vols, 2 * HX)]
    return jnp.concatenate(parts, axis=2)


def depth_slices(packed):
    vols = lax.axis_size("vol")
    moved = lax.all_to_all(packed, "vol", split_axis=1, concat_axis=1, tiled=True)
    return jnp.transpose(moved.reshape(C, vols, 8, HX), (0, 2, 1, 3)).reshape(C, 8 * NC)


def hop(array, pairs):
    return lax.ppermute(array, ("segment", "vol"), pairs)


def reduce_all(partial):
    vols = lax.axis_size("vol")
    part = partial.reshape(vols, partial.shape[0] // vols, partial.shape[1])
    part = lax.all_to_all(part, "vol", 0, 0)
    part = part.astype(F32).sum(axis=0).astype(BF)
    part = jnp.broadcast_to(part[None], (vols,) + part.shape)
    part = lax.all_to_all(part, "vol", 0, 0)
    return part.reshape(partial.shape)


def on_device(
    cotangent, labels, class_weight, inputs, fine_pre, pooled, coarse_pre, fine_filters, coarse_filters
):
    segments = lax.axis_size("segment")
    vols = lax.axis_size("vol")
    position = lax.axis_index("segment")
    pre = fine_pre[0].reshape(C, D * NF)
    head_edge = EDGE + NF
    at = lax.axis_index("vol")
    own, even, odd, spread = call(
        functools.partial(seed_kernel, vols - 1), SEED_VMEM,
        [(C, OWN), (C, head_edge), (C, head_edge), (NC, NF)], [SM, SM, VM, VM, VM], [], 10**9,
        (class_weight, at.astype(jnp.int32).reshape(1), cotangent.reshape(C, D * NF), labels, pre),
    )
    odd = lax.ppermute(odd, "vol", [(v, (v + (1 if v % 2 else -1)) % vols) for v in range(vols)])
    even = lax.ppermute(even, "vol", [(v, v ^ 1) for v in range(vols)])
    first_lo = jnp.where(at % 2 == 0, odd, even)
    first_hi = jnp.where(at % 2 == 0, even, odd)
    coarse_both = depth_slices(pack_rows(coarse_pre[0], pooled[0]))
    fine_w = filter_matrix(fine_filters[0])
    coarse_w = filter_matrix(coarse_filters[0])
    lo, hi = first_lo, first_hi
    keeps = ()
    for turn in range(segments - 1):
        s = segments - 1 - turn
        act = (position == s).astype(jnp.int32).reshape(1)
        up, down, own, *keeps = call(
            turn_kernel, TURN_VMEM,
            [(C, EDGE), (C, EDGE)],
            [SM, HB, VM, VM] + [HB] * (7 + len(keeps)),
            [
                pltpu.VMEM((C, 6 * NF), BF), pltpu.VMEM((3 * C, 9 * C), BF), pltpu.VMEM((C, OWN), BF),
                pltpu.SemaphoreType.DMA((4 + 2 * D,)), *front_scratch(),
            ],
            4 * 10**9,
            (act, own, lo, hi, first_lo, first_hi, pre, coarse_both, coarse_w, spread, fine_w, *keeps),
            ((C, OWN), (C, 6 * NF), (C, 6 * NC), (C, D * NF)),
            {11 + k: 3 + k for k in range(len(keeps))},
        )
        base, to = s * vols, (s - 1) * vols
        lo = hop(up, [(base + v, to + v + 1) for v in range(vols - 1)])
        hi = hop(down, [(base + v + 1, to + v) for v in range(vols - 1)])
        own = hop(own, [(base + v, to + v) for v in range(vols)])
    act = (position == 0).astype(jnp.int32).reshape(1)
    keep_gz, keep_coarse_gz, keep_grad = keeps
    partial, gz = call(
        last_kernel, LAST_VMEM,
        [(27 * C, 2 * C), (C, 6 * NF)],
        [SM, HB, VM, VM] + [HB] * 9,
        [
            pltpu.VMEM((C, D * NF), BF), pltpu.VMEM((C, 2 * NC), BF), pltpu.SemaphoreType.DMA((4,)),
            *front_scratch(),
        ],
        4 * 10**9,
        (
            act, own, lo, hi, first_lo, first_hi, pre, coarse_both, coarse_w, spread,
            keep_gz, keep_coarse_gz, inputs[0].reshape(C, D * NF),
        ),
    )
    (grad,) = call(
        grad_kernel, GRAD_VMEM, [], [SM, VM, VM, VM, HB],
        [pltpu.VMEM((C, D * NF), BF), pltpu.VMEM((18 * C, NF), BF), pltpu.SemaphoreType.DMA((1,))],
        2 * 10**9, (act, gz, own, fine_w, keep_grad), ((C, D * NF),), {4: 0},
    )
    total = reduce_all(partial)
    cells = D * vols * NF
    total = total.reshape(27, C, 2 * C).astype(F32)
    fine_total = total[:, :, :C] * (1.0 / math.sqrt(cells))
    coarse_total = total[:, :, C:] * (1.0 / math.sqrt(cells // 8))
    return grad.reshape(1, C, D, NF), fine_total[None], coarse_total[None]


def solution(mesh):
    return jax.shard_map(
        on_device,
        mesh=mesh,
        in_specs=(
            P(None, "vol", None),
            P("vol", None),
            P(),
            P("segment", None, "vol", None),
            P("segment", None, "vol", None),
            P("segment", None, "vol", None),
            P("segment", None, "vol", None),
            P("segment", None, None, None),
            P("segment", None, None, None),
        ),
        out_specs=(
            P("segment", None, "vol", None),
            P("segment", None, None, None),
            P("segment", None, None, None),
        ),
        check_vma=False,
    )
```
